32 devices in a mesh: dp: 8 (over z, core), mp: 4 (over y, x).
Axes of the slice: x: 2, y: 2, z: 4, core: 2. Of those that a mesh axis runs over, the one named last changes fastest.
Arguments:
- context: bfloat16 [2048, 4096], P('dp', 'mp'), parts along dimension 0, may hold values from -150 to 150
- w_out: bfloat16 [4096, 4096], P('mp'), may hold values from -0.09375 to 0.09375
- residual: bfloat16 [2048, 4096], P('dp', 'mp'), parts along dimension 0, may hold values from -150 to 150
- gain_temporal: float32 [4096], replicated, may hold values from 0.1 to 1.9
- w_in: bfloat16 [4096, 1024], P('mp'), may hold values from -0.09375 to 0.09375
- gain_depth: float32 [4, 1024], P('mp'), may hold values from 0.1 to 1.9
- w_depth: bfloat16 [4, 1024, 512], P('mp'), may hold values from -0.1875 to 0.1875
- cotangent: bfloat16 [4, 2048, 512], P('mp', 'dp'), parts along dimension 1, may hold values from -6 to 6
Outputs:
- depth_act: bfloat16 [4, 2048, 512], P('mp', 'dp'), parts along dimension 1
- grad_residual: bfloat16 [2048, 4096], P('dp', 'mp'), parts along dimension 0
- grad_context: bfloat16 [2048, 4096], P('dp', 'mp'), parts along dimension 0
The draws below stay inside these ranges and needn't reach their ends.
There are 8 independent parts, one for each index of `dp`. The reference program is written for one: setup_inputs(seed, part) draws one part's arguments, and reference() takes and returns one part's arrays. A program takes and returns all parts, laid end to end along the dimension named above; an argument that names none is the same for every part. Nothing has to cross between parts.
All inputs are finite; a program needn't handle non-finite values.
Results may differ from the reference program's by a relative error of at most 0.0058.
Values may be sent and summed in bfloat16 or wider, within the bound.
No kernel may reach another device: no remote copies, remote signals or barrier semaphores. Data moves between devices by JAX's collectives and lax.ppermute only.
A program may use at most 64 MiB of HBM per device.

```python
import jax
import jax.numpy as jnp
from jax import lax

D = 4096
DD = 1024
CTX = 4096
DQ = 512
F = 256
CODEBOOKS = 4


def scaled_field(key, rows, cols):
    keys = jax.random.split(key, 3)
    ramp = 10.0 ** (jnp.arange(cols, dtype=jnp.float32) / (cols - 1))
    col_scale = ramp * jnp.exp(jax.random.uniform(keys[1], (cols,), jnp.float32, -0.35, 0.35))
    row_scale = 10.0 ** jax.random.uniform(keys[0], (rows, 1), jnp.float32)
    base = jnp.clip(jax.random.normal(keys[2], (rows, cols), jnp.float32), -5.0, 5.0)
    return jnp.clip(0.2 * base * row_scale * col_scale, -150.0, 150.0)


def draw_context(key, part):
    return scaled_field(jax.random.fold_in(key, 11), F, CTX).astype(jnp.bfloat16)


def draw_residual(key, part):
    return scaled_field(jax.random.fold_in(key, 23), F, D).astype(jnp.bfloat16)


def level_of(key, shape, cuts, smallest, high):
    def one(axis_at, blocks):
        steps = jax.random.uniform(jax.random.fold_in(jax.random.fold_in(key, 6), axis_at), (blocks,), jnp.float32, smallest / len(cuts), high / len(cuts))
        return jnp.repeat(jnp.exp(steps), shape[axis_at] // blocks).reshape((-1,) + (1,) * (len(shape) - axis_at - 1))

    factor_of = one(*cuts[0])
    for cut in cuts[1:]:
        factor_of = factor_of * one(*cut)
    return factor_of


def centred(own_key, extent, scale, reach, shards=(), kind=jnp.bfloat16):
    level = level_of(own_key, extent, shards, -0.22, 0.18) if shards else 1.0
    drawn = jax.random.normal(own_key, extent, jnp.float32) * scale * level
    return jnp.minimum(jnp.maximum(drawn, -reach), reach).astype(kind)


def setup_inputs(seed: int = 0, part: int = 0) -> dict:
    splits = jax.random.split(jax.random.key(seed), 9)
    part_keys = jax.random.split(jax.random.fold_in(splits[8], part), 9)
    context = draw_context(jax.random.fold_in(jax.random.fold_in(splits[8], part), 71), part)
    w_out = centred(splits[1], (CTX, D), CTX ** -0.5, 0.09375, ((0, 4),))
    residual = draw_residual(jax.random.fold_in(jax.random.fold_in(splits[8], part), 71), part)
    gain_temporal = jnp.clip(1.0 + 0.18 * jax.random.normal(splits[3], (D,), jnp.float32), 0.1, 1.9)
    w_in = centred(splits[4], (D, DD), D ** -0.5, 0.09375, ((0, 4),))
    gain_depth = jnp.clip(1.0 + 0.18 * jax.random.normal(splits[5], (CODEBOOKS, DD), jnp.float32), 0.1, 1.9)
    w_depth = centred(splits[6], (CODEBOOKS, DD, DQ), DD ** -0.5, 0.1875, ((0, 4),))
    cotangent = centred(part_keys[7], (CODEBOOKS, F, DQ), 1.0, 6.0, ((0, 4),))
    return dict(context=context, w_out=w_out, residual=residual, gain_temporal=gain_temporal, w_in=w_in, gain_depth=gain_depth, w_depth=w_depth, cotangent=cotangent)


def norm_back(values, recip, gain, upstream):
    scaled = gain * upstream
    inner = lax.optimization_barrier(jnp.mean(values * scaled, axis=-1, keepdims=True))
    return recip * scaled - values * recip * recip * recip * inner

def reference(context, w_out, residual, gain_temporal, w_in, gain_depth, w_depth, cotangent):
    head_total = jnp.dot(context, w_out, preferred_element_type=jnp.float32)
    state = residual.astype(jnp.float32) + head_total
    recip = lax.rsqrt(lax.optimization_barrier(jnp.mean(state * state, axis=-1, keepdims=True)) + 1e-05)
    normed = (state * recip * gain_temporal).astype(jnp.bfloat16)
    depth_in = jnp.dot(normed, w_in, preferred_element_type=jnp.float32)
    urecip = lax.rsqrt(lax.optimization_barrier(jnp.mean(depth_in * depth_in, axis=-1, keepdims=True)) + 1e-05)
    gains = gain_depth[:, None, :]
    latent = (depth_in[None] * urecip[None] * gains).astype(jnp.bfloat16)
    depth_act = jnp.einsum('kfd,kde->kfe', latent.astype(jnp.float32), w_depth.astype(jnp.float32)).astype(jnp.bfloat16)
    dlatent = jnp.einsum('kfe,kde->kfd', cotangent.astype(jnp.float32), w_depth.astype(jnp.float32))
    dinput = norm_back(depth_in[None], urecip[None], gains, dlatent)
    du_total = lax.optimization_barrier(jnp.sum(dinput, axis=0)).astype(jnp.bfloat16)
    dnormed = jnp.dot(du_total, w_in.T, preferred_element_type=jnp.float32)
    grad_residual = norm_back(state, recip, gain_temporal, dnormed).astype(jnp.bfloat16)
    grad_context = jnp.dot(grad_residual, w_out.T, preferred_element_type=jnp.float32).astype(jnp.bfloat16)
    return (depth_act, grad_residual, grad_context)
```

```python
import jax
import jax.numpy as jnp
from jax import lax
from jax.sharding import PartitionSpec as P

EPS = 1e-05


def contract_last(left, right):
    return lax.dot_general(
        left, right, (((1,), (1,)), ((), ())), preferred_element_type=jnp.float32
    )


def local(n, context, w_out, residual, gain_temporal, w_in, gain_depth, w_depth, cotangent):
    bf16, f32 = jnp.bfloat16, jnp.float32
    me = lax.axis_index("mp")
    frames, width = residual.shape
    half = width // 2
    share = frames // n
    features = width * n
    depth = w_in.shape[1]
    bits = [1 << i for i in range(n.bit_length() - 1)]
    orders = (bits, bits[::-1])

    def swap(value, mask):
        return lax.ppermute(value, "mp", [(i, i ^ mask) for i in range(n)])

    def block_of(mask, side):
        return ((me ^ mask) * 2 + side) * half

    def w_out_cols(mask, side):
        return lax.dynamic_slice_in_dim(w_out, block_of(mask, side), half, 1)

    def rows_of(value, mask):
        return lax.dynamic_slice_in_dim(value, (me ^ mask) * share, share, 0)

    def sum_rows(value, kept):
        total = rows_of(kept, 0).astype(f32)
        for mask in range(n - 1, 0, -1):
            total = total + swap(rows_of(value, mask), mask).astype(f32)
        return total

    def gather_rows(own):
        whole = jnp.zeros((frames,) + own.shape[1:], own.dtype)
        parts = [(0, own)] + [(mask, swap(own, mask)) for mask in range(n - 1, 0, -1)]
        for mask, part in parts:
            whole = lax.dynamic_update_slice_in_dim(whole, part, (me ^ mask) * share, 0)
        return whole

    upstream = gain_depth[0] * contract_last(cotangent[0], w_depth[0])
    up_own = sum_rows(upstream.astype(bf16), upstream).astype(bf16)
    up_full = gather_rows(up_own).astype(f32)

    gains, state = [], []
    for side, order in enumerate(orders):
        total = {
            mask: jnp.dot(context, w_out_cols(mask, side), preferred_element_type=f32)
            for mask in range(n - 1, -1, -1)
        }
        left = list(total)
        for bit in order:
            for mask in [k for k in left if k & bit]:
                total[mask ^ bit] = total[mask ^ bit] + swap(
                    total[mask].astype(bf16), bit
                ).astype(f32)
            left = [k for k in left if not k & bit]
        state.append(residual[:, side * half : (side + 1) * half].astype(f32) + total[0])
        gains.append(lax.dynamic_slice_in_dim(gain_temporal, block_of(0, side), half, 0))

    squares = sum(jnp.sum(s * s, axis=1, keepdims=True) for s in state)
    high = squares.astype(bf16)
    low = (squares - high.astype(f32)).astype(bf16)
    raw = sum(
        jnp.dot((s * g).astype(bf16), w_in[i * half : (i + 1) * half], preferred_element_type=f32)
        for i, (s, g) in enumerate(zip(state, gains))
    )
    tail = jnp.concatenate([high, low, jnp.zeros((frames, 126), bf16)], axis=1)
    sent = jnp.concatenate([raw.astype(bf16), tail], axis=1)
    own = sum_rows(sent, sent)
    sq = own[:, depth : depth + 1] + own[:, depth + 1 : depth + 2]
    high = sq.astype(bf16)
    low = (sq - high.astype(f32)).astype(bf16)
    own = jnp.concatenate(
        [own[:, :depth].astype(bf16), high, low, jnp.zeros((share, 126), bf16)], axis=1
    )
    got = gather_rows(own)
    raw = got[:, :depth].astype(f32)
    squares = got[:, depth : depth + 1].astype(f32) + got[:, depth + 1 : depth + 2].astype(f32)

    recip = lax.rsqrt(squares / features + EPS)
    depth_in = raw * recip
    urecip = lax.rsqrt(jnp.mean(depth_in * depth_in, axis=-1, keepdims=True) + EPS)
    inner = jnp.mean(depth_in * up_full, axis=-1, keepdims=True)
    du = (urecip * up_full - depth_in * (urecip * urecip * urecip * inner)).astype(bf16)
    dot_du = jnp.sum(du.astype(f32) * depth_in, axis=1, keepdims=True) / recip
    back = recip * recip * recip * (dot_du / features)

    grad = []
    for side in range(2):
        dnormed = contract_last(du, w_in[side * half : (side + 1) * half])
        grad.append((recip * gains[side] * dnormed - state[side] * back).astype(bf16))

    grad_context = jnp.zeros((frames, w_out.shape[0]), f32)
    for side, order in enumerate(orders):
        have = {0: grad[side]}
        for bit in order:
            for mask in list(have):
                have[mask ^ bit] = swap(have[mask], bit)
        for mask, block in have.items():
            grad_context = grad_context + contract_last(block, w_out_cols(mask, side))

    latent = (depth_in * urecip * gain_depth[0]).astype(bf16)
    depth_act = jnp.dot(latent, w_depth[0], preferred_element_type=f32).astype(bf16)
    return (depth_act[None], jnp.concatenate(grad, axis=1), grad_context.astype(bf16))


def solution(mesh):
    in_specs = (
        P("dp", "mp"),
        P("mp", None),
        P("dp", "mp"),
        P(),
        P("mp", None),
        P("mp", None),
        P("mp", None, None),
        P("mp", "dp", None),
    )
    out_specs = (P("mp", "dp", None), P("dp", "mp"), P("dp", "mp"))
    n = mesh.shape["mp"]

    def run(*args):
        return local(n, *args)

    return jax.shard_map(run, mesh=mesh, in_specs=in_specs, out_specs=out_specs, check_vma=False)
```

```python
import functools

import jax
import jax.numpy as jnp
from jax import lax
from jax.experimental import pallas as pl
from jax.experimental.pallas import tpu as pltpu
from jax.sharding import PartitionSpec as P

EPS = 1e-05
LANES = 128
bf16, f32 = jnp.bfloat16, jnp.float32
VMEM = pl.BlockSpec(memory_space=pltpu.VMEM)
ANY = pl.BlockSpec(memory_space=pl.ANY)


def contract_last(left, right):
    return lax.dot_general(
        left, right, (((1,), (1,)), ((), ())), preferred_element_type=f32
    )


def call(body, outs, ins, in_specs, scratch=(), flops=0, name=None):
    moved = sum(a.size * a.dtype.itemsize for a in ins) // 4
    return pl.pallas_call(
        body,
        out_shape=[jax.ShapeDtypeStruct(s, d) for s, d in outs],
        in_specs=in_specs,
        out_specs=[VMEM] * len(outs),
        scratch_shapes=list(scratch),
        compiler_params=pltpu.CompilerParams(vmem_limit_bytes=16 * 2**20),
        cost_estimate=pl.CostEstimate(flops=flops, bytes_accessed=moved, transcendentals=0),
        name=name,
    )(*ins)


def high_low(total):
    high = total.astype(bf16)
    low = (total - high.astype(f32)).astype(bf16)
    lane = lax.broadcasted_iota(jnp.int32, (total.shape[0], LANES), 1)
    return jnp.where(lane < LANES // 2, high.astype(f32), low.astype(f32)).astype(bf16)


def from_high_low(block):
    return block[:, :1] + block[:, LANES // 2 : LANES // 2 + 1]


def upstream_kernel(n, share, cot, w_depth, gain_depth, *refs):
    outs, whole = refs[:n], refs[n]
    me = lax.axis_index("mp")
    whole[...] = gain_depth[...] * contract_last(cot[...], w_depth[...])
    for mask, out in enumerate(outs):
        rows = pl.ds(pl.multiple_of((me ^ mask) * share, share), share)
        out[...] = whole[rows, :].astype(out.dtype)


def project_kernel(items, half, context, w_out, *refs):
    count = sum(k for _, _, k in items)
    adds, outs = refs[:count], refs[count : count + len(items)]
    buf, sems = refs[count + len(items) :]
    me = lax.axis_index("mp")
    copies = []
    for i, (mask, side, _) in enumerate(items):
        start = pl.multiple_of(((me ^ mask) * 2 + side) * half, half)
        copies.append(
            pltpu.make_async_copy(w_out.at[:, pl.ds(start, half)], buf.at[i], sems.at[i])
        )
        copies[-1].start()
    at = 0
    for i, (_, _, k) in enumerate(items):
        copies[i].wait()
        total = jnp.dot(context[...], buf[i], preferred_element_type=f32)
        for add in adds[at : at + k]:
            total = total + add[...].astype(f32)
        at += k
        outs[i][...] = total.astype(outs[i].dtype)


def state_kernel(n, share, adds_per_side, gain, w_in, *refs):
    count = 2 * adds_per_side
    adds, (state, *outs), raw = refs[:count], refs[count : count + 1 + n], refs[count + 1 + n]
    me = lax.axis_index("mp")
    frames, width = state.shape
    half = width // 2
    depth = w_in.shape[1]
    for side in range(2):
        mine = adds[side * adds_per_side : (side + 1) * adds_per_side]
        total = mine[0][...]
        for add in mine[1:]:
            total = total + add[...].astype(f32)
        state[:, side * half : (side + 1) * half] = total
    value = state[...]
    gains = gain[:, pl.ds(pl.multiple_of(me * width, width), width)]
    raw[:, :depth] = jnp.dot((value * gains).astype(bf16), w_in[...], preferred_element_type=f32)
    raw[:, depth:] = jnp.broadcast_to(
        jnp.sum(value * value, axis=1, keepdims=True), (frames, LANES)
    )
    for mask, out in enumerate(outs):
        rows = pl.ds(pl.multiple_of((me ^ mask) * share, share), share)
        if mask == 0:
            out[...] = raw[rows, :]
        else:
            out[:, :depth] = raw[rows, :depth].astype(bf16)
            out[:, depth:] = high_low(raw[rows, depth:][:, :1])


def sum_kernel(n, own, *refs):
    out = refs[-1]
    total = own[...]
    for ref in refs[:-1]:
        total = total + ref[...].astype(f32)
    out[...] = total.astype(bf16)


def sum_state_kernel(n, depth, own, *refs):
    out = refs[-1]
    total = own[:, :depth]
    squares = own[:, depth : depth + 1]
    for ref in refs[:-1]:
        total = total + ref[:, :depth].astype(f32)
        squares = squares + from_high_low(ref[:, depth:].astype(f32))
    out[:, :depth] = total.astype(bf16)
    out[:, depth:] = high_low(squares)


def back_kernel(n, share, features, gain, gain_depth, w_in, state, *refs):
    raws, ups = refs[:n], refs[n : 2 * n]
    latent, grad, *halves = refs[2 * n : 2 * n + 4]
    du, recips, backs = refs[2 * n + 4 :]
    me = lax.axis_index("mp")
    width = state.shape[1]
    depth = w_in.shape[1]
    half = width // 2
    for mask in range(n):
        rows = pl.ds(pl.multiple_of((me ^ mask) * share, share), share)
        raw = raws[mask][:, :depth].astype(f32)
        squares = from_high_low(raws[mask][:, depth:].astype(f32))
        up = ups[mask][...].astype(f32)
        recip = lax.rsqrt(squares / features + EPS)
        depth_in = raw * recip
        urecip = lax.rsqrt(jnp.mean(depth_in * depth_in, axis=1, keepdims=True) + EPS)
        inner = jnp.mean(depth_in * up, axis=1, keepdims=True)
        part = (urecip * up - depth_in * (urecip * urecip * urecip * inner)).astype(bf16)
        du[rows, :] = part
        dot_du = jnp.sum(part.astype(f32) * depth_in, axis=1, keepdims=True) / recip
        recips[rows, :] = jnp.broadcast_to(recip, (share, LANES))
        backs[rows, :] = jnp.broadcast_to(
            recip * recip * recip * (dot_du / features), (share, LANES)
        )
        latent[rows, :] = (depth_in * urecip * gain_depth[...]).astype(bf16)
    gains = gain[:, pl.ds(pl.multiple_of(me * width, width), width)]
    for side in range(2):
        cols = slice(side * half, (side + 1) * half)
        dnormed = contract_last(du[...], w_in[cols, :])
        value = (
            recips[:, :1] * (gains[:, cols] * dnormed) - state[:, cols] * backs[:, :1]
        ).astype(bf16)
        halves[side][...] = value
        grad[:, cols] = value


def act_kernel(latent, w_depth, out):
    out[...] = jnp.dot(latent[...], w_depth[...], preferred_element_type=f32).astype(bf16)


def context_kernel(items, half, first, w_out, *refs):
    blocks = refs[: len(items)]
    before = None if first else refs[len(items)]
    out, buf, sems = refs[-3:]
    me = lax.axis_index("mp")
    copies = []
    for i, (mask, side) in enumerate(items):
        start = pl.multiple_of(((me ^ mask) * 2 + side) * half, half)
        copies.append(
            pltpu.make_async_copy(w_out.at[:, pl.ds(start, half)], buf.at[i], sems.at[i])
        )
        copies[-1].start()
    total = None if first else before[...]
    for i in range(len(items)):
        copies[i].wait()
        part = contract_last(blocks[i][...], buf[i])
        total = part if total is None else total + part
    out[...] = total.astype(out.dtype)


def local(n, context, w_out, residual, gain_temporal, w_in, gain_depth, w_depth, cotangent):
    frames, width = residual.shape
    half = width // 2
    share = frames // n
    features = width * n
    heads = w_out.shape[0]
    depth, act = w_depth.shape[1:]
    log = n.bit_length() - 1
    bits = [1 << i for i in range(log)]
    orders = (bits, bits[::-1])
    gain = gain_temporal[None, :]

    def mirror(mask):
        return sum(1 << (log - 1 - i) for i in range(log) if mask >> i & 1)

    pairs = sorted(range(n), key=lambda k: (-k.bit_count(), k))
    pairs = [((k, 0), (mirror(k), 1)) for k in pairs]

    def swap(value, mask):
        return lax.ppermute(value, "mp", [(i, i ^ mask) for i in range(n)])

    def exchange(values):
        return [swap(values[mask], mask) for mask in range(n - 1, 0, -1)]

    def gather(own):
        got = {mask: swap(own, mask) for mask in range(n - 1, 0, -1)}
        return [own] + [got[mask] for mask in range(1, n)]

    ups = call(
        functools.partial(upstream_kernel, n, share),
        [((share, depth), f32 if mask == 0 else bf16) for mask in range(n)],
        [cotangent[0], w_depth[0], gain_depth],
        [VMEM] * 3,
        [pltpu.VMEM((frames, depth), f32)],
        flops=2 * frames * depth * act,
        name="upstream",
    )

    def project(items, addends, dtype):
        listed = [a for adds in addends for a in adds]
        return call(
            functools.partial(
                project_kernel, [(m, s, len(a)) for (m, s), a in zip(items, addends)], half
            ),
            [((frames, half), dtype)] * len(items),
            [context, w_out] + listed,
            [VMEM, ANY] + [VMEM] * len(listed),
            [
                pltpu.VMEM((len(items), heads, half), bf16),
                pltpu.SemaphoreType.DMA((len(items),)),
            ],
            flops=2 * frames * heads * half * len(items),
            name="project",
        )

    arrived = {}
    for pair in pairs[:-1]:
        addends = []
        for mask, side in pair:
            order = orders[side]
            phase = min(i for i, bit in enumerate(order) if mask & bit)
            addends.append([arrived[mask ^ order[i], side] for i in range(phase)])
        sent = project(pair, addends, bf16)
        for (mask, side), value in zip(pair, sent):
            bit = next(bit for bit in orders[side] if mask & bit)
            arrived[mask, side] = swap(value, bit)
    kept = project(
        pairs[-1], [[residual[:, s * half : (s + 1) * half]] for s in range(2)], f32
    )

    up_own = call(
        functools.partial(sum_kernel, n),
        [((share, depth), bf16)],
        [ups[0]] + exchange(ups),
        [VMEM] * n,
        name="sum_upstream",
    )[0]
    up_parts = gather(up_own)

    adds = [[kept[side]] + [arrived[bit, side] for bit in orders[side]] for side in range(2)]
    state, *raws = call(
        functools.partial(state_kernel, n, share, 1 + log),
        [((frames, width), f32)]
        + [((share, depth + LANES), f32 if mask == 0 else bf16) for mask in range(n)],
        [gain, w_in] + adds[0] + adds[1],
        [VMEM] * (4 + 2 * log),
        [pltpu.VMEM((frames, depth + LANES), f32)],
        flops=2 * frames * width * depth,
        name="state",
    )
    raw_own = call(
        functools.partial(sum_state_kernel, n, depth),
        [((share, depth + LANES), bf16)],
        [raws[0]] + exchange(raws),
        [VMEM] * n,
        name="sum_state",
    )[0]
    raw_parts = gather(raw_own)

    latent, grad_residual, *grads = call(
        functools.partial(back_kernel, n, share, features),
        [((frames, depth), bf16), ((frames, width), bf16)] + [((frames, half), bf16)] * 2,
        [gain, gain_depth, w_in, state] + raw_parts + up_parts,
        [VMEM] * (4 + 2 * n),
        [
            pltpu.VMEM((frames, depth), bf16),
            pltpu.VMEM((frames, LANES), f32),
            pltpu.VMEM((frames, LANES), f32),
        ],
        flops=2 * frames * width * depth,
        name="back",
    )

    blocks = {}
    for side, order in enumerate(orders):
        blocks[0, side] = grads[side]
        have = [0]
        for bit in order:
            for mask in list(have):
                blocks[mask ^ bit, side] = swap(blocks[mask, side], bit)
                have.append(mask ^ bit)

    depth_act = call(
        act_kernel,
        [((frames, act), bf16)],
        [latent, w_depth[0]],
        [VMEM] * 2,
        flops=2 * frames * depth * act,
        name="act",
    )[0]

    total = None
    for i, pair in enumerate(pairs[::-1]):
        ins = [w_out] + [blocks[key] for key in pair] + ([] if total is None else [total])
        total = call(
            functools.partial(context_kernel, pair, half, total is None),
            [((frames, heads), bf16 if i == n - 1 else f32)],
            ins,
            [ANY] + [VMEM] * (len(ins) - 1),
            [
                pltpu.VMEM((len(pair), heads, half), bf16),
                pltpu.SemaphoreType.DMA((len(pair),)),
            ],
            flops=2 * frames * heads * half * len(pair),
            name="grad_context",
        )[0]
    return (depth_act[None], grad_residual, total)


def solution(mesh):
    in_specs = (
        P("dp", "mp"),
        P("mp", None),
        P("dp", "mp"),
        P(),
        P("mp", None),
        P("mp", None),
        P("mp", None, None),
        P("mp", "dp", None),
    )
    out_specs = (P("mp", "dp", None), P("dp", "mp"), P("dp", "mp"))
    n = mesh.shape["mp"]

    def run(*args):
        return local(n, *args)

    return jax.shard_map(run, mesh=mesh, in_specs=in_specs, out_specs=out_specs, check_vma=False)
```

```python
import functools

import jax
import jax.numpy as jnp
from jax import lax
from jax.experimental import pallas as pl
from jax.experimental.pallas import tpu as pltpu
from jax.sharding import PartitionSpec as P

EPS = 1e-05
LANES = 128
SQ = 16
EARLY = 16
bf16, f32 = jnp.bfloat16, jnp.float32
VMEM = pl.BlockSpec(memory_space=pltpu.VMEM)
HBM = pl.BlockSpec(memory_space=pltpu.HBM)


def contract_last(left, right):
    return lax.dot_general(
        left, right, (((1,), (1,)), ((), ())), preferred_element_type=f32
    )


def call(body, outs, ins, in_specs, scratch=(), flops=0, name=None, limit=16):
    ins = [
        pltpu.with_memory_space_constraint(a, pltpu.HBM) if spec is HBM else a
        for a, spec in zip(ins, in_specs)
    ]
    moved = sum(a.size * a.dtype.itemsize for a in ins) // 4
    return pl.pallas_call(
        body,
        out_shape=[jax.ShapeDtypeStruct(s, d) for s, d in outs],
        in_specs=in_specs,
        out_specs=[VMEM] * len(outs),
        scratch_shapes=list(scratch),
        compiler_params=pltpu.CompilerParams(vmem_limit_bytes=limit * 2**20),
        cost_estimate=pl.CostEstimate(flops=flops, bytes_accessed=moved, transcendentals=0),
        name=name,
    )(*ins)


def put_squares(out, at, squares):
    frames = squares.shape[1]
    high = squares.astype(bf16).astype(f32)
    both = jnp.concatenate([high, squares - high], axis=0).astype(bf16)
    out[at : at + SQ, :frames] = both
    if frames < out.shape[1]:
        out[at : at + SQ, frames:] = jnp.zeros((SQ, out.shape[1] - frames), bf16)


def get_squares(ref, at, frames):
    both = ref[at : at + SQ, :frames].astype(f32)
    return both[: SQ // 2] + both[SQ // 2 :]


def rows_of(mask, share):
    return pl.ds(pl.multiple_of((lax.axis_index("mp") ^ mask) * share, share), share)


def block_of(mask, side, half):
    start = ((lax.axis_index("mp") ^ mask) * 2 + side) * half
    return pl.ds(pl.multiple_of(start, half), half)


def put_block(out, product, up, adds, mask, side, share):
    frames, half = product.shape
    wide = up.shape[1] // 2
    for add in adds:
        product = product + add[:frames, :].astype(f32)
    out[:frames, :] = product.astype(bf16)
    for c in range(wide // half):
        rows = slice(frames + c * share, frames + (c + 1) * share)
        col = side * wide + c * half
        part = up[rows_of(mask, share), col : col + half]
        for add in adds:
            part = part + add[rows, :].astype(f32)
        out[rows, :] = part.astype(bf16)


def head_kernel(items, share, cot, w_depth, gain_hbm, context, w_out, *refs):
    outs, up = refs[: len(items)], refs[len(items)]
    cot_buf, depth_buf, gain_depth, context_buf, buf, sems = refs[len(items) + 1 :]
    half = buf.shape[2]
    pairs = [(cot, cot_buf), (w_depth, depth_buf), (gain_hbm, gain_depth)]
    pairs += [(context, context_buf)]
    pairs += [(w_out.at[:, block_of(m, s, half)], buf.at[i]) for i, (m, s) in enumerate(items)]
    copies = [pltpu.make_async_copy(a, b, sems.at[i]) for i, (a, b) in enumerate(pairs)]
    for copy in copies:
        copy.start()
    for copy in copies[:3]:
        copy.wait()
    up[...] = gain_depth[...] * contract_last(cot_buf[...], depth_buf[...])
    copies[3].wait()
    for i, (mask, side) in enumerate(items):
        copies[4 + i].wait()
        product = jnp.dot(context_buf[...], buf[i], preferred_element_type=f32)
        put_block(outs[i], product, up, [], mask, side, share)


def project_kernel(items, share, context, w_out, up, *refs):
    count = sum(k for _, _, k in items)
    adds, outs = refs[:count], refs[count:]
    half = outs[0].shape[1]
    at = 0
    for i, (mask, side, k) in enumerate(items):
        product = jnp.dot(
            context[...], w_out[:, block_of(mask, side, half)], preferred_element_type=f32
        )
        put_block(outs[i], product, up, adds[at : at + k], mask, side, share)
        at += k


def early_kernel(items, share, context, w_out, up, *refs):
    outs, (buf, sems) = refs[: len(items)], refs[len(items) :]
    half = buf.shape[2]
    copies = [
        pltpu.make_async_copy(w_out.at[:, block_of(m, s, half)], buf.at[i], sems.at[i])
        for i, (m, s) in enumerate(items)
    ]
    for copy in copies:
        copy.start()
    for i, (mask, side) in enumerate(items):
        copies[i].wait()
        product = jnp.dot(context[...], buf[i], preferred_element_type=f32)
        put_block(outs[i], product, up, [], mask, side, share)


def keep_kernel(context, w_out, residual, out):
    half = out.shape[1] // 2
    for side in range(2):
        cols = slice(side * half, (side + 1) * half)
        out[:, cols] = residual[:, cols].astype(f32) + jnp.dot(
            context[...], w_out[:, block_of(0, side, half)], preferred_element_type=f32
        )


def state_kernel(log, share, gain, w_in, up, kept, *refs):
    adds = refs[: 2 * log]
    state, raw, squares, *sends = refs[2 * log :]
    frames, width = state.shape
    half = width // 2
    wide = raw.shape[1] // 2
    for side in range(2):
        cols = slice(side * half, (side + 1) * half)
        total = kept[:, cols]
        for add in adds[side * log : (side + 1) * log]:
            total = total + add[:frames, :].astype(f32)
        state[:, cols] = total
    value = state[...]
    gains = gain[:, pl.ds(pl.multiple_of(lax.axis_index("mp") * width, width), width)]
    raw[...] = jnp.dot((value * gains).astype(bf16), w_in[...], preferred_element_type=f32)
    column = jnp.sum(value * value, axis=1, keepdims=True)
    row = jnp.transpose(jnp.broadcast_to(column, (frames, LANES)))[: SQ // 2]
    for side, send in enumerate(sends):
        squares[side] = row
        send[:frames, :] = raw[:, side * wide : (side + 1) * wide].astype(bf16)
        put_squares(send, frames, row)
        for c in range(wide // half):
            col = side * wide + c * half
            part = up[rows_of(0, share), col : col + half]
            for add in adds[side * log : (side + 1) * log]:
                part = part + add[frames + c * share : frames + (c + 1) * share, :].astype(f32)
            send[frames + SQ :, c * half : (c + 1) * half] = part.astype(bf16)


def reduce_kernel(raw, squares, *refs):
    sent, got = refs[:2], refs[2:4]
    raw_out, squares_out, *sends = refs[4:]
    frames, depth = raw.shape
    wide = depth // 2
    for side in range(2):
        cols = slice(side * wide, (side + 1) * wide)
        total = raw[:, cols] + got[side][:frames, :].astype(f32)
        raw_out[:, cols] = total
        sends[side][:frames, :] = total.astype(bf16)
        row = squares[side] + get_squares(got[side], frames, frames)
        squares_out[side] = row
        put_squares(sends[side], frames, row)
        first = frames + SQ
        held = sent[side].shape[0] - first
        sends[side][first : first + held, :] = sent[side][first:, :]
        sends[side][first + held :, :] = got[side][first:, :]


def back_kernel(haves, share, features, gain, gain_depth, w_in, state, raw, squares, *refs):
    sent, got = refs[:2], refs[2:4]
    latent, grad, *halves = refs[4:8]
    up, du = refs[8:]
    frames, width = state.shape
    depth = w_in.shape[1]
    half, wide = width // 2, depth // 2
    first = frames + SQ
    for side in range(2):
        held = sent[side].shape[0] - first
        for i, mask in enumerate(haves[side]):
            ref, at = (sent[side], i * share) if i * share < held else (got[side], i * share - held)
            up[rows_of(mask, share), side * wide : (side + 1) * wide] = ref[
                first + at : first + at + share, :
            ]
    row = squares[0] + get_squares(got[0], frames, frames)
    recip = jnp.transpose(
        jnp.broadcast_to(lax.rsqrt(row[:1] / features + EPS), (LANES, frames))
    )[:, :1]
    back = []
    step = 64 if frames % 64 == 0 else frames
    for at in range(0, frames, step):
        rows = slice(at, at + step)
        total = [
            raw[rows, side * wide : (side + 1) * wide] + got[side][rows, :].astype(f32)
            for side in range(2)
        ]
        depth_in = jnp.concatenate(total, axis=1) * recip[rows]
        grads = up[rows, :].astype(f32)
        urecip = lax.rsqrt(jnp.mean(depth_in * depth_in, axis=1, keepdims=True) + EPS)
        inner = jnp.mean(depth_in * grads, axis=1, keepdims=True)
        part = (urecip * grads - depth_in * (urecip * urecip * urecip * inner)).astype(bf16)
        du[rows, :] = part
        dot_du = jnp.sum(part.astype(f32) * depth_in, axis=1, keepdims=True) / recip[rows]
        back.append(recip[rows] * recip[rows] * recip[rows] * (dot_du / features))
        latent[rows, :] = (depth_in * urecip * gain_depth[...]).astype(bf16)
    back = jnp.concatenate(back, axis=0)
    gains = gain[:, pl.ds(pl.multiple_of(lax.axis_index("mp") * width, width), width)]
    for side in range(2):
        cols = slice(side * half, (side + 1) * half)
        dnormed = contract_last(du[...], w_in[cols, :])
        value = (recip * (gains[:, cols] * dnormed) - state[:, cols] * back).astype(bf16)
        halves[side][...] = value
        grad[:, cols] = value


def act_kernel(latent, w_depth, out):
    out[...] = jnp.dot(latent[...], w_depth[...], preferred_element_type=f32).astype(bf16)


def context_kernel(items, w_out, *refs):
    blocks, rest, out = refs[: len(items)], refs[len(items) : -1], refs[-1]
    total = rest[0][...] if rest else None
    for (mask, side), block in zip(items, blocks):
        half = block.shape[1]
        part = contract_last(block[...], w_out[:, block_of(mask, side, half)])
        total = part if total is None else total + part
    out[...] = total.astype(out.dtype)


def local(n, context, w_out, residual, gain_temporal, w_in, gain_depth, w_depth, cotangent):
    frames, width = residual.shape
    half = width // 2
    share = frames // n
    features = width * n
    heads = w_out.shape[0]
    depth, act = w_depth.shape[1:]
    wide = depth // 2
    log = n.bit_length() - 1
    bits = [1 << i for i in range(log)]
    orders = (bits, bits[::-1])
    gain = gain_temporal[None, :]
    block = (frames + share * (wide // half), half)

    def mirror(mask):
        return sum(1 << (log - 1 - i) for i in range(log) if mask >> i & 1)

    pairs = sorted(range(n), key=lambda k: (-k.bit_count(), k))
    pairs = [((k, 0), (mirror(k), 1)) for k in pairs]

    def swap(value, mask):
        return lax.ppermute(value, "mp", [(i, i ^ mask) for i in range(n)])

    first = pairs[0]
    *blocks, up = call(
        functools.partial(head_kernel, first, share),
        [(block, bf16)] * 2 + [((frames, depth), f32)],
        [cotangent[0], w_depth[0], gain_depth, context, w_out],
        [HBM] * 5,
        [
            pltpu.VMEM((frames, act), bf16),
            pltpu.VMEM((depth, act), bf16),
            pltpu.VMEM((1, depth), f32),
            pltpu.VMEM(context.shape, bf16),
            pltpu.VMEM((2, heads, half), bf16),
            pltpu.SemaphoreType.DMA((6,)),
        ],
        flops=2 * frames * (depth * act + heads * width),
        name="head",
        limit=EARLY,
    )
    arrived = {}
    for pair in pairs[:-1]:
        if pair is not first:
            addends = []
            for mask, side in pair:
                order = orders[side]
                phase = min(i for i, bit in enumerate(order) if mask & bit)
                addends.append([arrived[mask ^ order[i], side] for i in range(phase)])
            listed = [a for adds in addends for a in adds]
            if not listed:
                blocks = call(
                    functools.partial(early_kernel, pair, share),
                    [(block, bf16)] * 2,
                    [context, w_out, up],
                    [VMEM, HBM, VMEM],
                    [pltpu.VMEM((2, heads, half), bf16), pltpu.SemaphoreType.DMA((2,))],
                    flops=2 * frames * heads * width,
                    name="early",
                    limit=EARLY,
                )
            else:
                blocks = call(
                    functools.partial(
                        project_kernel, [(m, s, len(a)) for (m, s), a in zip(pair, addends)], share
                    ),
                    [(block, bf16)] * 2,
                    [context, w_out, up] + listed,
                    [VMEM] * (3 + len(listed)),
                    flops=2 * frames * heads * width,
                    name="project",
                )
        for (mask, side), value in zip(pair, blocks):
            bit = next(bit for bit in orders[side] if mask & bit)
            arrived[mask, side] = swap(value, bit)
    kept = call(
        keep_kernel,
        [((frames, width), f32)],
        [context, w_out, residual],
        [VMEM] * 3,
        flops=2 * frames * heads * width,
        name="keep",
    )[0]

    state, raw, squares, *sends = call(
        functools.partial(state_kernel, log, share),
        [((frames, width), f32), ((frames, depth), f32), ((2, SQ // 2, frames), f32)]
        + [((frames + SQ + share, wide), bf16)] * 2,
        [gain, w_in, up, kept]
        + [arrived[bit, side] for side in range(2) for bit in orders[side]],
        [VMEM] * (4 + 2 * log),
        flops=2 * frames * width * depth,
        name="state",
    )

    haves = [[0], [0]]
    for i in range(log):
        got = [swap(sends[side], orders[side][i]) for side in range(2)]
        haves = [have + [k ^ orders[s][i] for k in have] for s, have in enumerate(haves)]
        if i < log - 1:
            raw, squares, *sends = call(
                reduce_kernel,
                [(raw.shape, f32), (squares.shape, f32)]
                + [((frames + SQ + share * len(haves[0]), wide), bf16)] * 2,
                [raw, squares] + list(sends) + got,
                [VMEM] * 6,
                name="reduce",
            )

    latent, grad_residual, *grads = call(
        functools.partial(back_kernel, haves, share, features),
        [((frames, depth), bf16), ((frames, width), bf16)] + [((frames, half), bf16)] * 2,
        [gain, gain_depth, w_in, state, raw, squares] + list(sends) + got,
        [VMEM] * 10,
        [pltpu.VMEM((frames, depth), bf16)] * 2,
        flops=2 * frames * width * depth,
        name="back",
    )

    blocks = {}
    for side, order in enumerate(orders):
        blocks[0, side] = grads[side]
        have = [0]
        for bit in order:
            for mask in list(have):
                blocks[mask ^ bit, side] = swap(blocks[mask, side], bit)
                have.append(mask ^ bit)

    depth_act = call(
        act_kernel,
        [((frames, act), bf16)],
        [latent, w_depth[0]],
        [VMEM] * 2,
        flops=2 * frames * depth * act,
        name="act",
    )[0]

    total = None
    for i, pair in enumerate(pairs[::-1]):
        ins = [w_out] + [blocks[key] for key in pair] + ([] if total is None else [total])
        total = call(
            functools.partial(context_kernel, pair),
            [((frames, heads), bf16 if i == n - 1 else f32)],
            ins,
            [VMEM] * len(ins),
            flops=2 * frames * heads * width,
            name="grad_context",
        )[0]
    return (depth_act[None], grad_residual, total)


def solution(mesh):
    in_specs = (
        P("dp", "mp"),
        P("mp", None),
        P("dp", "mp"),
        P(),
        P("mp", None),
        P("mp", None),
        P("mp", None, None),
        P("mp", "dp", None),
    )
    out_specs = (P("mp", "dp", None), P("dp", "mp"), P("dp", "mp"))
    n = mesh.shape["mp"]

    def run(*args):
        return local(n, *args)

    return jax.shard_map(run, mesh=mesh, in_specs=in_specs, out_specs=out_specs, check_vma=False)
```

```python
import functools

import jax
import jax.numpy as jnp
from jax import lax
from jax.experimental import pallas as pl
from jax.experimental.pallas import tpu as pltpu
from jax.sharding import PartitionSpec as P

EPS = 1e-05
LANES = 128
SQ = 16
bf16, f32 = jnp.bfloat16, jnp.float32
VMEM = pl.BlockSpec(memory_space=pltpu.VMEM)
HBM = pl.BlockSpec(memory_space=pltpu.HBM)

COST = pl.CostEstimate(flops=20 * 10**9, bytes_accessed=60 * 10**6, transcendentals=0)
FREE = pl.CostEstimate(flops=0, bytes_accessed=0, transcendentals=0)


def contract_last(left, right):
    return lax.dot_general(
        left, right, (((1,), (1,)), ((), ())), preferred_element_type=f32
    )


def mirror(mask, log):
    return sum(1 << (log - 1 - i) for i in range(log) if mask >> i & 1)


def call(body, outs, ins, in_specs=None, scratch=(), name=None, out_specs=None, after=None, cost=COST):
    in_specs = in_specs or [VMEM] * len(ins)
    ins = [
        pltpu.with_memory_space_constraint(a, pltpu.HBM) if spec is HBM else a
        for a, spec in zip(ins, in_specs)
    ]
    count = len(ins)
    kernel = body
    if after is not None:
        ins = ins + [after]
        in_specs = in_specs + [pl.BlockSpec(memory_space=pl.ANY)]

        def kernel(*refs):
            body(*refs[:count], *refs[count + 1 :])

    return pl.pallas_call(
        kernel,
        out_shape=[jax.ShapeDtypeStruct(s, d) for s, d in outs],
        in_specs=in_specs,
        out_specs=out_specs or [VMEM] * len(outs),
        scratch_shapes=list(scratch),
        compiler_params=pltpu.CompilerParams(vmem_limit_bytes=16 * 2**20),
        cost_estimate=cost,
        name=name,
    )(*ins)


def put_squares(out, at, squares):
    frames = squares.shape[1]
    high = squares.astype(bf16).astype(f32)
    both = jnp.concatenate([high, squares - high], axis=0).astype(bf16)
    out[at : at + SQ, :frames] = both
    if frames < out.shape[1]:
        out[at : at + SQ, frames:] = jnp.zeros((SQ, out.shape[1] - frames), bf16)


def get_squares(ref, at, frames):
    both = ref[at : at + SQ, :frames].astype(f32)
    return both[: SQ // 2] + both[SQ // 2 :]


def owner(mask):
    return lax.axis_index("mp") ^ mask


def span(start, size):
    return pl.ds(pl.multiple_of(start * size, size), size)


def cols_of(mask, side, half):
    return span(owner(mask) * 2 + side, half)


def put_block(log, share, out, product, up, adds, mask, side):
    frames, half = product.shape
    wide = up.shape[1] // 2
    for add in adds:
        product = product + add[:frames, :].astype(f32)
    out[:frames, :] = product.astype(bf16)
    for c in range(wide // half):
        col = side * wide + c * half
        part = up[span(owner(mask), share), col : col + half]
        rows = slice(frames + c * share, frames + (c + 1) * share)
        for add in adds:
            part = part + add[rows, :].astype(f32)
        out[rows, :] = part.astype(bf16)


def head_kernel(log, share, items, cot, w_depth, gain_hbm, context, w_out, *refs):
    outs, up = refs[: len(items)], refs[len(items)]
    cot_buf, depth_buf, gain_depth, context_buf, buf, sems = refs[len(items) + 1 :]
    half = buf.shape[2]
    pairs = [(cot, cot_buf), (w_depth, depth_buf), (gain_hbm, gain_depth)]
    pairs += [(context, context_buf)]
    for i, (mask, side) in enumerate(items):
        pairs.append((w_out.at[:, cols_of(mask, side, half)], buf.at[i]))
    copies = [pltpu.make_async_copy(a, b, sems.at[i]) for i, (a, b) in enumerate(pairs)]
    for copy in copies:
        copy.start()
    for copy in copies[:3]:
        copy.wait()
    up[...] = gain_depth[...] * contract_last(cot_buf[...], depth_buf[...])
    copies[3].wait()
    for i, (mask, side) in enumerate(items):
        copies[4 + i].wait()
        product = jnp.dot(context_buf[...], buf[i], preferred_element_type=f32)
        put_block(log, share, outs[i], product, up, [], mask, side)


def early_kernel(log, share, items, context, w_out, up, *refs):
    outs, (buf, sems) = refs[: len(items)], refs[len(items) :]
    half = buf.shape[2]
    copies = []
    for i, (mask, side) in enumerate(items):
        cols = cols_of(mask, side, half)
        copies.append(pltpu.make_async_copy(w_out.at[:, cols], buf.at[i], sems.at[i]))
        copies[-1].start()
    for i, (mask, side) in enumerate(items):
        copies[i].wait()
        product = jnp.dot(context[...], buf[i], preferred_element_type=f32)
        put_block(log, share, outs[i], product, up, [], mask, side)


def project_kernel(log, share, items, context, w_out, up, *refs):
    adds, outs = refs[: -len(items)], refs[-len(items) :]
    half = outs[0].shape[1]
    at = 0
    for (mask, side, count), out in zip(items, outs):
        product = jnp.dot(
            context[...], w_out[:, cols_of(mask, side, half)], preferred_element_type=f32
        )
        put_block(log, share, out, product, up, adds[at : at + count], mask, side)
        at += count


def keep_kernel(context, w_out, residual, out):
    out[...] = residual[...].astype(f32) + jnp.dot(
        context[...],
        w_out[:, span(lax.axis_index("mp"), out.shape[1])],
        preferred_element_type=f32,
    )


def state_kernel(log, share, gain, w_in, up, kept, *refs):
    adds, (state, raw, squares, *sends) = refs[: 2 * log], refs[2 * log :]
    frames, width = state.shape
    half = width // 2
    wide = raw.shape[1] // 2
    for side in range(2):
        cols = slice(side * half, (side + 1) * half)
        total = kept[:, cols]
        for add in adds[side * log : (side + 1) * log]:
            total = total + add[:frames, :].astype(f32)
        state[:, cols] = total
    value = state[...]
    gains = gain[:, span(lax.axis_index("mp"), width)]
    raw[...] = jnp.dot((value * gains).astype(bf16), w_in[...], preferred_element_type=f32)
    column = jnp.sum(value * value, axis=1, keepdims=True)
    row = jnp.transpose(jnp.broadcast_to(column, (frames, LANES)))[: SQ // 2]
    for side, send in enumerate(sends):
        squares[side] = row
        send[:frames, :] = raw[:, side * wide : (side + 1) * wide].astype(bf16)
        put_squares(send, frames, row)
        for c in range(wide // half):
            col = side * wide + c * half
            part = up[span(lax.axis_index("mp"), share), col : col + half]
            for add in adds[side * log : (side + 1) * log]:
                at = frames + c * share
                part = part + add[at : at + share, :].astype(f32)
            send[frames + SQ :, c * half : (c + 1) * half] = part.astype(bf16)


def reduce_kernel(raw, squares, *refs):
    sent, got, (raw_out, squares_out, *sends) = refs[:2], refs[2:4], refs[4:]
    frames, depth = raw.shape
    wide = depth // 2
    for side in range(2):
        cols = slice(side * wide, (side + 1) * wide)
        total = raw[:, cols] + got[side][:frames, :].astype(f32)
        raw_out[:, cols] = total
        sends[side][:frames, :] = total.astype(bf16)
        row = squares[side] + get_squares(got[side], frames, frames)
        squares_out[side] = row
        put_squares(sends[side], frames, row)
        first = frames + SQ
        held = sent[side].shape[0] - first
        sends[side][first : first + held, :] = sent[side][first:, :]
        sends[side][first + held :, :] = got[side][first:, :]


def depth_rows(raw, got, rows):
    wide = raw.shape[1] // 2
    return jnp.concatenate(
        [
            raw[rows, side * wide : (side + 1) * wide] + got[side][rows, :].astype(f32)
            for side in range(2)
        ],
        axis=1,
    )


def recip_of(squares, got, frames, features):
    row = squares[0] + get_squares(got[0], frames, frames)
    return jnp.transpose(
        jnp.broadcast_to(lax.rsqrt(row[:1] / features + EPS), (LANES, frames))
    )[:, :1]


def back_kernel(log, haves, share, features, gain, w_in, state, raw, squares, *refs):
    sent, got, (*grads, up, du) = refs[:2], refs[2:4], refs[4:]
    frames, width = state.shape
    half, wide = width // 2, raw.shape[1] // 2
    first = frames + SQ
    for side in range(2):
        held = sent[side].shape[0] - first
        for i, mask in enumerate(haves[side]):
            at = i * share
            ref, at = (sent[side], at) if at < held else (got[side], at - held)
            up[span(owner(mask), share), side * wide : (side + 1) * wide] = ref[
                first + at : first + at + share, :
            ]
    recip = recip_of(squares, got, frames, features)
    back = []
    step = 64 if frames % 64 == 0 else frames
    for at in range(0, frames, step):
        rows = slice(at, at + step)
        depth_in = depth_rows(raw, got, rows) * recip[rows]
        upstream = up[rows, :].astype(f32)
        urecip = lax.rsqrt(jnp.mean(depth_in * depth_in, axis=1, keepdims=True) + EPS)
        inner = jnp.mean(depth_in * upstream, axis=1, keepdims=True)
        part = urecip * upstream - depth_in * (urecip * urecip * urecip * inner)
        part = part.astype(bf16)
        du[rows, :] = part
        dot_du = jnp.sum(part.astype(f32) * depth_in, axis=1, keepdims=True) / recip[rows]
        back.append(recip[rows] * recip[rows] * recip[rows] * (dot_du / features))
    back = jnp.concatenate(back, axis=0)
    gains = gain[:, span(lax.axis_index("mp"), width)]
    for side, grad in enumerate(grads):
        cols = slice(side * half, (side + 1) * half)
        dnormed = contract_last(du[...], w_in[cols, :])
        grad[...] = (recip * (gains[:, cols] * dnormed) - state[:, cols] * back).astype(bf16)


def act_kernel(features, gain_depth, w_depth, raw, squares, *refs):
    got, grads, (out, grad_out, latent) = refs[:2], refs[2:4], refs[4:]
    frames = raw.shape[0]
    half = grads[0].shape[1]
    for side in range(2):
        grad_out[:, side * half : (side + 1) * half] = grads[side][...]
    recip = recip_of(squares, got, frames, features)
    step = 64 if frames % 64 == 0 else frames
    for at in range(0, frames, step):
        rows = slice(at, at + step)
        depth_in = depth_rows(raw, got, rows) * recip[rows]
        urecip = lax.rsqrt(jnp.mean(depth_in * depth_in, axis=1, keepdims=True) + EPS)
        latent[rows, :] = (depth_in * urecip * gain_depth[...]).astype(bf16)
    out[...] = jnp.dot(latent[...], w_depth[...], preferred_element_type=f32).astype(bf16)


def context_kernel(log, items, w_out, *refs):
    blocks, rest, out = refs[: len(items)], refs[len(items) : -1], refs[-1]
    total = rest[0][...]
    for (mask, side), block in zip(items, blocks):
        part = contract_last(block[...], w_out[:, cols_of(mask, side, block.shape[1])])
        total = total + part
    out[...] = total


def own_context_kernel(log, w_out, first, second, out, *copies):
    total = None
    for side, block in enumerate((first, second)):
        half = block.shape[1]
        part = contract_last(block[...], w_out[:, cols_of(0, side, half)])
        total = part if total is None else total + part
        copies[side][...] = block[...]
    out[...] = total


def last_kernel(log, items, w_out, *refs):
    blocks, (total, out, buf, sems) = refs[: len(items)], refs[len(items) :]
    step = total.shape[1] // 2
    copies = []
    for k in range(2):
        rows = slice(k * step, (k + 1) * step)
        value = total[:, rows]
        for (mask, side), block in zip(items, blocks):
            value = value + contract_last(
                block[...], w_out[rows, cols_of(mask, side, block.shape[1])]
            )
        buf[:, rows] = value.astype(bf16)
        copies.append(pltpu.make_async_copy(buf.at[:, rows], out.at[:, rows], sems.at[k]))
        copies[-1].start()
    for copy in copies:
        copy.wait()


def local(n, context, w_out, residual, gain_temporal, w_in, gain_depth, w_depth, cotangent):
    frames, width = residual.shape
    half = width // 2
    share = frames // n
    features = width * n
    heads = w_out.shape[0]
    depth, act = w_depth.shape[1:]
    wide = depth // 2
    log = n.bit_length() - 1
    bits = [1 << i for i in range(log)]
    orders = (bits, bits[::-1])
    gain = gain_temporal[None, :]
    block = ((frames + share * (wide // half), half), bf16)

    def swap(value, bit):
        return lax.ppermute(value, "mp", [(i, i ^ bit) for i in range(n)])

    def phase_of(mask, side):
        return min(i for i, bit in enumerate(orders[side]) if mask & bit)

    masks = sorted(range(1, n), key=lambda k: (-k.bit_count(), k))
    pairs = [((k, 0), (mirror(k, log), 1)) for k in masks]

    arrived = {}
    for pair in pairs:
        adds = [
            [arrived[mask ^ bit, side] for bit in orders[side][: phase_of(mask, side)]]
            for mask, side in pair
        ]
        if pair is pairs[0]:
            *values, up = call(
                functools.partial(head_kernel, log, share, pair),
                [block] * 2 + [((frames, depth), f32)],
                [cotangent[0], w_depth[0], gain_depth, context, w_out],
                [HBM] * 5,
                [
                    pltpu.VMEM((frames, act), bf16),
                    pltpu.VMEM((depth, act), bf16),
                    pltpu.VMEM((1, depth), f32),
                    pltpu.VMEM(context.shape, bf16),
                    pltpu.VMEM((2, heads, half), bf16),
                    pltpu.SemaphoreType.DMA((6,)),
                ],
                name="head",
            )
        elif not adds[0]:
            values = call(
                functools.partial(early_kernel, log, share, pair),
                [block] * 2,
                [context, w_out, up],
                [VMEM, HBM, VMEM],
                [pltpu.VMEM((2, heads, half), bf16), pltpu.SemaphoreType.DMA((2,))],
                name="early",
            )
        else:
            items = [(mask, side, len(a)) for (mask, side), a in zip(pair, adds)]
            values = call(
                functools.partial(project_kernel, log, share, items),
                [block] * 2,
                [context, w_out, up] + adds[0] + adds[1],
                name="project",
            )
        for (mask, side), value in zip(pair, values):
            arrived[mask, side] = swap(value, orders[side][phase_of(mask, side)])
    kept = call(
        keep_kernel,
        [((frames, width), f32)],
        [context, w_out, residual],
        name="keep",
        after=values[0],
    )[0]

    state, raw, squares, *sends = call(
        functools.partial(state_kernel, log, share),
        [((frames, width), f32), ((frames, depth), f32), ((2, SQ // 2, frames), f32)]
        + [((frames + SQ + share, wide), bf16)] * 2,
        [gain, w_in, up, kept] + [arrived[bit, side] for side in range(2) for bit in orders[side]],
        name="state",
    )
    haves = [[0], [0]]
    for i in range(log):
        got = [swap(sends[side], orders[side][i]) for side in range(2)]
        haves = [have + [k ^ orders[s][i] for k in have] for s, have in enumerate(haves)]
        if i < log - 1:
            raw, squares, *sends = call(
                reduce_kernel,
                [(raw.shape, f32), (squares.shape, f32)]
                + [((frames + SQ + share * len(haves[0]), wide), bf16)] * 2,
                [raw, squares] + list(sends) + got,
                name="reduce",
            )
    grads = call(
        functools.partial(back_kernel, log, haves, share, features),
        [((frames, half), bf16)] * 2,
        [gain, w_in, state, raw, squares] + list(sends) + got,
        scratch=[pltpu.VMEM((frames, depth), bf16)] * 2,
        name="back",
    )

    total, *again = call(
        functools.partial(own_context_kernel, log),
        [((frames, heads), f32)] + [((frames, half), bf16)] * 2,
        [w_out] + list(grads),
        name="grad_context",
    )
    blocks = {(0, side): grads[side] for side in range(2)}
    for i in range(log):
        for k in range(1 << i):
            for side, order in enumerate(orders):
                mask = haves[side][k]
                value = again[side] if i and not k else blocks[mask, side]
                blocks[mask ^ order[i], side] = swap(value, order[i])

    depth_act, grad_residual = call(
        functools.partial(act_kernel, features),
        [((frames, act), bf16), ((frames, width), bf16)],
        [gain_depth, w_depth[0], raw, squares] + got + list(grads),
        scratch=[pltpu.VMEM((frames, depth), bf16)],
        name="act",
    )
    keys = [((haves[0][k], 0), (haves[1][k], 1)) for k in range(n)]
    for pair in keys[1:-1]:
        total = call(
            functools.partial(context_kernel, log, pair),
            [((frames, heads), f32)],
            [w_out] + [blocks[key] for key in pair] + [total],
            name="grad_context",
        )[0]
    grad_context = call(
        functools.partial(last_kernel, log, keys[-1]),
        [((frames, heads), bf16)],
        [w_out] + [blocks[key] for key in keys[-1]] + [total],
        scratch=[pltpu.VMEM((frames, heads), bf16), pltpu.SemaphoreType.DMA((2,))],
        name="grad_context",
        out_specs=[HBM],
    )[0]
    return (depth_act[None], grad_residual, grad_context)


def solution(mesh):
    in_specs = (
        P("dp", "mp"),
        P("mp", None),
        P("dp", "mp"),
        P(),
        P("mp", None),
        P("mp", None),
        P("mp", None, None),
        P("mp", "dp", None),
    )
    out_specs = (P("mp", "dp", None), P("dp", "mp"), P("dp", "mp"))
    n = mesh.shape["mp"]

    def run(*args):
        return local(n, *args)

    return jax.shard_map(run, mesh=mesh, in_specs=in_specs, out_specs=out_specs, check_vma=False)
```

```python
import functools

import jax
import jax.numpy as jnp
from jax import lax
from jax.experimental import pallas as pl
from jax.experimental.pallas import tpu as pltpu
from jax.sharding import PartitionSpec as P

EPS = 1e-05
LANES = 128
SQ = 16
bf16, f32 = jnp.bfloat16, jnp.float32
VMEM = pl.BlockSpec(memory_space=pltpu.VMEM)
HBM = pl.BlockSpec(memory_space=pltpu.HBM)

COST = pl.CostEstimate(flops=20 * 10**9, bytes_accessed=60 * 10**6, transcendentals=0)
FREE = pl.CostEstimate(flops=0, bytes_accessed=0, transcendentals=0)


def contract_last(left, right):
    return lax.dot_general(
        left, right, (((1,), (1,)), ((), ())), preferred_element_type=f32
    )


def mirror(mask, log):
    return sum(1 << (log - 1 - i) for i in range(log) if mask >> i & 1)


def call(body, outs, ins, in_specs=None, scratch=(), name=None, out_specs=None, after=None, cost=COST):
    in_specs = in_specs or [VMEM] * len(ins)
    ins = [
        pltpu.with_memory_space_constraint(a, pltpu.HBM) if spec is HBM else a
        for a, spec in zip(ins, in_specs)
    ]
    count = len(ins)
    kernel = body
    if after is not None:
        ins = ins + [after]
        in_specs = in_specs + [pl.BlockSpec(memory_space=pl.ANY)]

        def kernel(*refs):
            body(*refs[:count], *refs[count + 1 :])

    return pl.pallas_call(
        kernel,
        out_shape=[jax.ShapeDtypeStruct(s, d) for s, d in outs],
        in_specs=in_specs,
        out_specs=out_specs or [VMEM] * len(outs),
        scratch_shapes=list(scratch),
        compiler_params=pltpu.CompilerParams(vmem_limit_bytes=16 * 2**20),
        cost_estimate=cost,
        name=name,
    )(*ins)


def put_squares(out, at, squares):
    frames = squares.shape[1]
    high = squares.astype(bf16).astype(f32)
    both = jnp.concatenate([high, squares - high], axis=0).astype(bf16)
    out[at : at + SQ, :frames] = both
    if frames < out.shape[1]:
        out[at : at + SQ, frames:] = jnp.zeros((SQ, out.shape[1] - frames), bf16)


def get_squares(ref, at, frames):
    both = ref[at : at + SQ, :frames].astype(f32)
    return both[: SQ // 2] + both[SQ // 2 :]


def owner(mask):
    return lax.axis_index("mp") ^ mask


def span(start, size):
    return pl.ds(pl.multiple_of(start * size, size), size)


def cols_of(mask, side, half):
    return span(owner(mask) * 2 + side, half)


def upstream_kernel(share, masks, cot, w_depth, gain_hbm, *refs):
    *outs, up = refs[:-4]
    cot_buf, depth_buf, gain_depth, sems = refs[-4:]
    pairs = [(cot, cot_buf), (w_depth, depth_buf), (gain_hbm, gain_depth)]
    copies = [pltpu.make_async_copy(a, b, sems.at[i]) for i, (a, b) in enumerate(pairs)]
    for copy in copies:
        copy.start()
    for copy in copies:
        copy.wait()
    up[...] = gain_depth[...] * contract_last(cot_buf[...], depth_buf[...])
    wide = up.shape[1] // 2
    for side, out in enumerate(outs):
        for i, mask in enumerate(masks[side]):
            out[i * share : (i + 1) * share, :] = up[
                span(owner(mask), share), side * wide : (side + 1) * wide
            ].astype(bf16)


def share_of(share, up, mask, side, got, place, adds, frames, half, c):
    wide = up.shape[1] // 2
    cols = slice(c * half, (c + 1) * half)
    part = up[span(owner(mask), share), side * wide + c * half : side * wide + (c + 1) * half]
    part = part + got[place * share : (place + 1) * share, cols].astype(f32)
    for add in adds:
        part = part + add[frames + c * share : frames + (c + 1) * share, :].astype(f32)
    return part


def project_kernel(share, items, context, w_out, *refs):
    outs, refs = refs[-len(items) :], refs[: -len(items)]
    half = outs[0].shape[1]
    frames = context.shape[0]
    at = 3
    for (mask, side, count, place), out in zip(items, outs):
        product = jnp.dot(
            context[...], w_out[:, cols_of(mask, side, half)], preferred_element_type=f32
        )
        adds = refs[at : at + count]
        at += count
        for add in adds:
            product = product + add[:frames, :].astype(f32)
        out[:frames, :] = product.astype(bf16)
        if not count:
            continue
        up, got = refs[0], refs[1 + side]
        for c in range(up.shape[1] // 2 // half):
            rows = slice(frames + c * share, frames + (c + 1) * share)
            out[rows, :] = share_of(
                share, up, mask, side, got, place, adds[1:], frames, half, c
            ).astype(bf16)


def keep_kernel(context, w_out, residual, out):
    out[...] = residual[...].astype(f32) + jnp.dot(
        context[...],
        w_out[:, span(lax.axis_index("mp"), out.shape[1])],
        preferred_element_type=f32,
    )


def state_kernel(log, share, places, gain, w_in, up, kept, *refs):
    got, adds = refs[:2], refs[2 : 2 + 2 * log]
    state, raw, squares, *sends = refs[2 + 2 * log :]
    frames, width = state.shape
    half = width // 2
    wide = raw.shape[1] // 2
    for side in range(2):
        cols = slice(side * half, (side + 1) * half)
        total = kept[:, cols]
        for add in adds[side * log : (side + 1) * log]:
            total = total + add[:frames, :].astype(f32)
        state[:, cols] = total
    value = state[...]
    gains = gain[:, span(lax.axis_index("mp"), width)]
    raw[...] = jnp.dot((value * gains).astype(bf16), w_in[...], preferred_element_type=f32)
    column = jnp.sum(value * value, axis=1, keepdims=True)
    row = jnp.transpose(jnp.broadcast_to(column, (frames, LANES)))[: SQ // 2]
    for side, send in enumerate(sends):
        squares[side] = row
        send[:frames, :] = raw[:, side * wide : (side + 1) * wide].astype(bf16)
        put_squares(send, frames, row)
        late = adds[side * log + 1 : (side + 1) * log]
        for c in range(wide // half):
            send[frames + SQ :, c * half : (c + 1) * half] = share_of(
                share, up, 0, side, got[side], places[side], late, frames, half, c
            ).astype(bf16)


def reduce_kernel(raw, squares, *refs):
    sent, got, (raw_out, squares_out, *sends) = refs[:2], refs[2:4], refs[4:]
    frames, depth = raw.shape
    wide = depth // 2
    for side in range(2):
        cols = slice(side * wide, (side + 1) * wide)
        total = raw[:, cols] + got[side][:frames, :].astype(f32)
        raw_out[:, cols] = total
        sends[side][:frames, :] = total.astype(bf16)
        row = squares[side] + get_squares(got[side], frames, frames)
        squares_out[side] = row
        put_squares(sends[side], frames, row)
        first = frames + SQ
        held = sent[side].shape[0] - first
        sends[side][first : first + held, :] = sent[side][first:, :]
        sends[side][first + held :, :] = got[side][first:, :]


def depth_rows(raw, got, rows):
    wide = raw.shape[1] // 2
    return jnp.concatenate(
        [
            raw[rows, side * wide : (side + 1) * wide] + got[side][rows, :].astype(f32)
            for side in range(2)
        ],
        axis=1,
    )


def recip_of(squares, got, frames, features):
    row = squares[0] + get_squares(got[0], frames, frames)
    return jnp.transpose(
        jnp.broadcast_to(lax.rsqrt(row[:1] / features + EPS), (LANES, frames))
    )[:, :1]


def back_kernel(log, haves, share, features, gain, w_in, state, raw, squares, *refs):
    sent, got, (*grads, up, du) = refs[:2], refs[2:4], refs[4:]
    frames, width = state.shape
    half, wide = width // 2, raw.shape[1] // 2
    first = frames + SQ
    for side in range(2):
        held = sent[side].shape[0] - first
        for i, mask in enumerate(haves[side]):
            at = i * share
            ref, at = (sent[side], at) if at < held else (got[side], at - held)
            up[span(owner(mask), share), side * wide : (side + 1) * wide] = ref[
                first + at : first + at + share, :
            ]
    recip = recip_of(squares, got, frames, features)
    back = []
    step = 64 if frames % 64 == 0 else frames
    for at in range(0, frames, step):
        rows = slice(at, at + step)
        depth_in = depth_rows(raw, got, rows) * recip[rows]
        upstream = up[rows, :].astype(f32)
        urecip = lax.rsqrt(jnp.mean(depth_in * depth_in, axis=1, keepdims=True) + EPS)
        inner = jnp.mean(depth_in * upstream, axis=1, keepdims=True)
        part = urecip * upstream - depth_in * (urecip * urecip * urecip * inner)
        part = part.astype(bf16)
        du[rows, :] = part
        dot_du = jnp.sum(part.astype(f32) * depth_in, axis=1, keepdims=True) / recip[rows]
        back.append(recip[rows] * recip[rows] * recip[rows] * (dot_du / features))
    back = jnp.concatenate(back, axis=0)
    gains = gain[:, span(lax.axis_index("mp"), width)]
    for side, grad in enumerate(grads):
        cols = slice(side * half, (side + 1) * half)
        dnormed = contract_last(du[...], w_in[cols, :])
        grad[...] = (recip * (gains[:, cols] * dnormed) - state[:, cols] * back).astype(bf16)


def act_kernel(features, gain_depth, w_depth, raw, squares, *refs):
    got, grads, (out, grad_out, latent) = refs[:2], refs[2:4], refs[4:]
    frames = raw.shape[0]
    half = grads[0].shape[1]
    for side in range(2):
        grad_out[:, side * half : (side + 1) * half] = grads[side][...]
    recip = recip_of(squares, got, frames, features)
    step = 64 if frames % 64 == 0 else frames
    for at in range(0, frames, step):
        rows = slice(at, at + step)
        depth_in = depth_rows(raw, got, rows) * recip[rows]
        urecip = lax.rsqrt(jnp.mean(depth_in * depth_in, axis=1, keepdims=True) + EPS)
        latent[rows, :] = (depth_in * urecip * gain_depth[...]).astype(bf16)
    out[...] = jnp.dot(latent[...], w_depth[...], preferred_element_type=f32).astype(bf16)


def context_kernel(log, items, w_out, *refs):
    blocks, rest, out = refs[: len(items)], refs[len(items) : -1], refs[-1]
    total = rest[0][...]
    for (mask, side), block in zip(items, blocks):
        part = contract_last(block[...], w_out[:, cols_of(mask, side, block.shape[1])])
        total = total + part
    out[...] = total


def own_context_kernel(log, w_out, first, second, out, *copies):
    total = None
    for side, block in enumerate((first, second)):
        half = block.shape[1]
        part = contract_last(block[...], w_out[:, cols_of(0, side, half)])
        total = part if total is None else total + part
        copies[side][...] = block[...]
    out[...] = total


def last_kernel(log, mask, side, w_out, block, total, out, buf, sems):
    pieces = sems.shape[0]
    step = total.shape[1] // pieces
    copies = []
    for k in range(pieces):
        rows = slice(k * step, (k + 1) * step)
        part = contract_last(block[...], w_out[rows, cols_of(mask, side, block.shape[1])])
        buf[:, rows] = (total[:, rows] + part).astype(bf16)
        copies.append(pltpu.make_async_copy(buf.at[:, rows], out.at[:, rows], sems.at[k]))
        copies[-1].start()
    for copy in copies:
        copy.wait()


def local(n, context, w_out, residual, gain_temporal, w_in, gain_depth, w_depth, cotangent):
    frames, width = residual.shape
    half = width // 2
    share = frames // n
    features = width * n
    heads = w_out.shape[0]
    depth, act = w_depth.shape[1:]
    wide = depth // 2
    log = n.bit_length() - 1
    bits = [1 << i for i in range(log)]
    orders = (bits, bits[::-1])
    gain = gain_temporal[None, :]
    extra = share * (wide // half)

    def swap(value, bit):
        return lax.ppermute(value, "mp", [(i, i ^ bit) for i in range(n)])

    def phase_of(mask, side):
        return min(i for i, bit in enumerate(orders[side]) if mask & bit)

    masks = sorted(range(1, n), key=lambda k: (-k.bit_count(), k))
    pairs = [((k, 0), (mirror(k, log), 1)) for k in masks]

    first = [[mask for mask in range(1, n) if phase_of(mask, side) == 0] for side in range(2)]
    *values, up = call(
        functools.partial(upstream_kernel, share, first),
        [((share * n // 2, wide), bf16)] * 2 + [((frames, depth), f32)],
        [cotangent[0], w_depth[0], gain_depth],
        [HBM] * 3,
        [
            pltpu.VMEM((frames, act), bf16),
            pltpu.VMEM((depth, act), bf16),
            pltpu.VMEM((1, depth), f32),
            pltpu.SemaphoreType.DMA((3,)),
        ],
        name="upstream",
    )
    got_up = [swap(values[side], orders[side][0]) for side in range(2)]

    def place(mask, side):
        return first[side].index(mask ^ orders[side][0])

    arrived = {}
    token = up
    for pair in pairs:
        items, listed = [], []
        for mask, side in pair:
            phase = phase_of(mask, side)
            listed += [arrived[mask ^ bit, side] for bit in orders[side][:phase]]
            items.append((mask, side, phase, place(mask, side) if phase else 0))
        shape = ((frames + (extra if phase else 0), half), bf16)
        values = call(
            functools.partial(project_kernel, share, items),
            [shape] * 2,
            [context, w_out, up] + got_up + listed
            if listed
            else [context, w_out, up, gain, gain],
            name="project",
            after=token,
        )
        token = values[0]
        for (mask, side), value in zip(pair, values):
            arrived[mask, side] = swap(value, orders[side][phase_of(mask, side)])
    kept = call(
        keep_kernel,
        [((frames, width), f32)],
        [context, w_out, residual],
        name="keep",
        after=values[0],
    )[0]

    state, raw, squares, *sends = call(
        functools.partial(state_kernel, log, share, [place(0, side) for side in range(2)]),
        [((frames, width), f32), ((frames, depth), f32), ((2, SQ // 2, frames), f32)]
        + [((frames + SQ + share, wide), bf16)] * 2,
        [gain, w_in, up, kept]
        + got_up
        + [arrived[bit, side] for side in range(2) for bit in orders[side]],
        name="state",
    )
    haves = [[0], [0]]
    for i in range(log):
        got = [swap(sends[side], orders[side][i]) for side in range(2)]
        haves = [have + [k ^ orders[s][i] for k in have] for s, have in enumerate(haves)]
        if i < log - 1:
            raw, squares, *sends = call(
                reduce_kernel,
                [(raw.shape, f32), (squares.shape, f32)]
                + [((frames + SQ + share * len(haves[0]), wide), bf16)] * 2,
                [raw, squares] + list(sends) + got,
                name="reduce",
            )
    grads = call(
        functools.partial(back_kernel, log, haves, share, features),
        [((frames, half), bf16)] * 2,
        [gain, w_in, state, raw, squares] + list(sends) + got,
        scratch=[pltpu.VMEM((frames, depth), bf16)] * 2,
        name="back",
    )

    total, *again = call(
        functools.partial(own_context_kernel, log),
        [((frames, heads), f32)] + [((frames, half), bf16)] * 2,
        [w_out] + list(grads),
        name="grad_context",
    )
    blocks = {(0, side): grads[side] for side in range(2)}
    for i in range(log):
        for k in range(1 << i):
            for side, order in enumerate(orders):
                mask = haves[side][k]
                value = again[side] if i and not k else blocks[mask, side]
                blocks[mask ^ order[i], side] = swap(value, order[i])

    depth_act, grad_residual = call(
        functools.partial(act_kernel, features),
        [((frames, act), bf16), ((frames, width), bf16)],
        [gain_depth, w_depth[0], raw, squares] + got + list(grads),
        scratch=[pltpu.VMEM((frames, depth), bf16)],
        name="act",
    )
    keys = [((haves[0][k], 0), (haves[1][k], 1)) for k in range(n)]
    final = keys[-1][1]
    for pair in keys[1:-1] + [keys[-1][:1]]:
        total = call(
            functools.partial(context_kernel, log, pair),
            [((frames, heads), f32)],
            [w_out] + [blocks[key] for key in pair] + [total],
            name="grad_context",
        )[0]
    grad_context = call(
        functools.partial(last_kernel, log, *final),
        [((frames, heads), bf16)],
        [w_out, blocks[final], total],
        scratch=[pltpu.VMEM((frames, heads), bf16), pltpu.SemaphoreType.DMA((2,))],
        name="grad_context",
        out_specs=[HBM],
    )[0]
    return (depth_act[None], grad_residual, grad_context)


def solution(mesh):
    in_specs = (
        P("dp", "mp"),
        P("mp", None),
        P("dp", "mp"),
        P(),
        P("mp", None),
        P("mp", None),
        P("mp", None, None),
        P("mp", "dp", None),
    )
    out_specs = (P("mp", "dp", None), P("dp", "mp"), P("dp", "mp"))
    n = mesh.shape["mp"]

    def run(*args):
        return local(n, *args)

    return jax.shard_map(run, mesh=mesh, in_specs=in_specs, out_specs=out_specs, check_vma=False)
```

```python
import functools

import jax
import jax.numpy as jnp
from jax import lax
from jax.experimental import pallas as pl
from jax.experimental.pallas import tpu as pltpu
from jax.sharding import PartitionSpec as P

EPS = 1e-05
LANES = 128
SQ = 16
OUT_PIECES = 4
bf16, f32 = jnp.bfloat16, jnp.float32
VMEM = pl.BlockSpec(memory_space=pltpu.VMEM)
HBM = pl.BlockSpec(memory_space=pltpu.HBM)

COST = pl.CostEstimate(flops=20 * 10**9, bytes_accessed=60 * 10**6, transcendentals=0)
FREE = pl.CostEstimate(flops=0, bytes_accessed=0, transcendentals=0)


def contract_last(left, right):
    return lax.dot_general(
        left, right, (((1,), (1,)), ((), ())), preferred_element_type=f32
    )


def mirror(mask, log):
    return sum(1 << (log - 1 - i) for i in range(log) if mask >> i & 1)


def call(body, outs, ins, in_specs=None, scratch=(), name=None, out_specs=None, after=None, cost=COST):
    in_specs = in_specs or [VMEM] * len(ins)
    ins = [
        pltpu.with_memory_space_constraint(a, pltpu.HBM) if spec is HBM else a
        for a, spec in zip(ins, in_specs)
    ]
    count = len(ins)
    kernel = body
    if after is not None:
        ins = ins + [after]
        in_specs = in_specs + [pl.BlockSpec(memory_space=pl.ANY)]

        def kernel(*refs):
            body(*refs[:count], *refs[count + 1 :])

    return pl.pallas_call(
        kernel,
        out_shape=[jax.ShapeDtypeStruct(s, d) for s, d in outs],
        in_specs=in_specs,
        out_specs=out_specs or [VMEM] * len(outs),
        scratch_shapes=list(scratch),
        compiler_params=pltpu.CompilerParams(vmem_limit_bytes=16 * 2**20),
        cost_estimate=cost,
        name=name,
    )(*ins)


def put_squares(out, at, squares):
    frames = squares.shape[1]
    high = squares.astype(bf16).astype(f32)
    both = jnp.concatenate([high, squares - high], axis=0).astype(bf16)
    out[at : at + SQ, :frames] = both
    if frames < out.shape[1]:
        out[at : at + SQ, frames:] = jnp.zeros((SQ, out.shape[1] - frames), bf16)


def get_squares(ref, at, frames):
    both = ref[at : at + SQ, :frames].astype(f32)
    return both[: SQ // 2] + both[SQ // 2 :]


def owner(mask):
    return lax.axis_index("mp") ^ mask


def span(start, size):
    return pl.ds(pl.multiple_of(start * size, size), size)


def cols_of(mask, side, half):
    return span(owner(mask) * 2 + side, half)


def upstream_kernel(share, masks, cot, w_depth, gain_hbm, *refs):
    *outs, up = refs[:-4]
    cot_buf, depth_buf, gain_depth, sems = refs[-4:]
    pieces = sems.shape[0] - 2
    step = depth_buf.shape[0] // pieces
    pairs = [(cot, cot_buf), (gain_hbm, gain_depth)]
    for k in range(pieces):
        rows = pl.ds(k * step, step)
        pairs.append((w_depth.at[rows, :], depth_buf.at[rows, :]))
    copies = [pltpu.make_async_copy(a, b, sems.at[i]) for i, (a, b) in enumerate(pairs)]
    for copy in copies:
        copy.start()
    copies[0].wait()
    copies[1].wait()
    for k in range(pieces):
        copies[2 + k].wait()
        cols = slice(k * step, (k + 1) * step)
        up[:, cols] = gain_depth[:, cols] * contract_last(cot_buf[...], depth_buf[cols, :])
    wide = up.shape[1] // 2
    for side, out in enumerate(outs):
        for i, mask in enumerate(masks[side]):
            out[i * share : (i + 1) * share, :] = up[
                span(owner(mask), share), side * wide : (side + 1) * wide
            ].astype(bf16)


def put_shares(share, items, up, gots, outs, first):
    wide = up.shape[1] // 2
    for side, (rows, out) in enumerate(zip(items, outs)):
        for i, (mask, places) in enumerate(rows):
            part = up[span(owner(mask), share), side * wide : (side + 1) * wide]
            for phase, at in enumerate(places):
                part = part + gots[2 * phase + side][at : at + share, :].astype(f32)
            out[first + i * share : first + (i + 1) * share, :] = part.astype(bf16)


def shares_kernel(share, items, up, *refs):
    put_shares(share, items, up, refs[:-2], refs[-2:], 0)


def join_kernel(*refs):
    for side in range(2):
        first, second, out = refs[side], refs[2 + side], refs[4 + side]
        out[: first.shape[0], :] = first[...]
        out[first.shape[0] :, :] = second[...]


def project_kernel(share, items, riders, context, w_out, *refs):
    adds, outs = refs[: -len(items)], refs[-len(items) :]
    half = outs[0].shape[1]
    frames = context.shape[0]
    at = 0
    for (mask, side, count), out in zip(items, outs):
        product = jnp.dot(
            context[...], w_out[:, cols_of(mask, side, half)], preferred_element_type=f32
        )
        for add in adds[at : at + count]:
            product = product + add[:frames, :].astype(f32)
        out[:frames, :] = product.astype(bf16)
        at += count
    if riders:
        put_shares(share, riders, adds[at], adds[at + 1 :], outs[::-1], frames)


def keep_kernel(context, w_out, residual, out):
    out[...] = residual[...].astype(f32) + jnp.dot(
        context[...],
        w_out[:, span(lax.axis_index("mp"), out.shape[1])],
        preferred_element_type=f32,
    )


def state_kernel(log, gain, w_in, kept, *refs):
    adds, (state, raw, squares, *sends) = refs[: 2 * log], refs[2 * log :]
    frames, width = state.shape
    half = width // 2
    wide = raw.shape[1] // 2
    for side in range(2):
        cols = slice(side * half, (side + 1) * half)
        total = kept[:, cols]
        for add in adds[side * log : (side + 1) * log]:
            total = total + add[:frames, :].astype(f32)
        state[:, cols] = total
    value = state[...]
    gains = gain[:, span(lax.axis_index("mp"), width)]
    raw[...] = jnp.dot((value * gains).astype(bf16), w_in[...], preferred_element_type=f32)
    column = jnp.sum(value * value, axis=1, keepdims=True)
    row = jnp.transpose(jnp.broadcast_to(column, (frames, LANES)))[: SQ // 2]
    for side, send in enumerate(sends):
        send[:frames, :] = raw[:, side * wide : (side + 1) * wide].astype(bf16)
    squares[...] = row
    put_squares(sends[0], frames, row)


def reduce_kernel(raw, squares, *refs):
    got, (raw_out, squares_out, *sends) = refs[:2], refs[2:]
    frames, depth = raw.shape
    wide = depth // 2
    for side in range(2):
        cols = slice(side * wide, (side + 1) * wide)
        total = raw[:, cols] + got[side][:frames, :].astype(f32)
        raw_out[:, cols] = total
        sends[side][:frames, :] = total.astype(bf16)
    row = squares[...] + get_squares(got[0], frames, frames)
    squares_out[...] = row
    put_squares(sends[0], frames, row)


def depth_rows(raw, got, rows):
    wide = raw.shape[1] // 2
    return jnp.concatenate(
        [
            raw[rows, side * wide : (side + 1) * wide] + got[side][rows, :].astype(f32)
            for side in range(2)
        ],
        axis=1,
    )


def recip_of(squares, got, frames, features):
    row = squares[...] + get_squares(got[0], frames, frames)
    return jnp.transpose(
        jnp.broadcast_to(lax.rsqrt(row[:1] / features + EPS), (LANES, frames))
    )[:, :1]


def assemble_kernel(haves, share, *refs):
    sent, rest, up = refs[:2], refs[2:4], refs[4]
    wide = up.shape[1] // 2
    for side in range(2):
        held = sent[side].shape[0]
        for i, mask in enumerate(haves[side]):
            at = i * share
            ref, at = (sent[side], at) if at < held else (rest[side], at - held)
            up[span(owner(mask), share), side * wide : (side + 1) * wide] = ref[
                at : at + share, :
            ]


def back_kernel(features, gain, w_in, up, state, raw, squares, *refs):
    got, (*grads, du) = refs[:2], refs[2:]
    frames, width = state.shape
    half = width // 2
    recip = recip_of(squares, got, frames, features)
    back = []
    step = 64 if frames % 64 == 0 else frames
    for at in range(0, frames, step):
        rows = slice(at, at + step)
        depth_in = depth_rows(raw, got, rows) * recip[rows]
        upstream = up[rows, :].astype(f32)
        urecip = lax.rsqrt(jnp.mean(depth_in * depth_in, axis=1, keepdims=True) + EPS)
        inner = jnp.mean(depth_in * upstream, axis=1, keepdims=True)
        part = urecip * upstream - depth_in * (urecip * urecip * urecip * inner)
        part = part.astype(bf16)
        du[rows, :] = part
        dot_du = jnp.sum(part.astype(f32) * depth_in, axis=1, keepdims=True) / recip[rows]
        back.append(recip[rows] * recip[rows] * recip[rows] * (dot_du / features))
    back = jnp.concatenate(back, axis=0)
    gains = gain[:, span(lax.axis_index("mp"), width)]
    for side, grad in enumerate(grads):
        cols = slice(side * half, (side + 1) * half)
        dnormed = contract_last(du[...], w_in[cols, :])
        grad[...] = (recip * (gains[:, cols] * dnormed) - state[:, cols] * back).astype(bf16)


def act_kernel(features, gain_depth, w_depth, raw, squares, *refs):
    got, grads, (out, grad_out, latent) = refs[:2], refs[2:4], refs[4:]
    frames = raw.shape[0]
    half = grads[0].shape[1]
    for side in range(2):
        grad_out[:, side * half : (side + 1) * half] = grads[side][...]
    recip = recip_of(squares, got, frames, features)
    step = 64 if frames % 64 == 0 else frames
    for at in range(0, frames, step):
        rows = slice(at, at + step)
        depth_in = depth_rows(raw, got, rows) * recip[rows]
        urecip = lax.rsqrt(jnp.mean(depth_in * depth_in, axis=1, keepdims=True) + EPS)
        latent[rows, :] = (depth_in * urecip * gain_depth[...]).astype(bf16)
    out[...] = jnp.dot(latent[...], w_depth[...], preferred_element_type=f32).astype(bf16)


def context_kernel(log, items, w_out, *refs):
    blocks, rest, out = refs[: len(items)], refs[len(items) : -1], refs[-1]
    total = rest[0][...]
    for (mask, side), block in zip(items, blocks):
        part = contract_last(block[...], w_out[:, cols_of(mask, side, block.shape[1])])
        total = total + part
    out[...] = total


def own_context_kernel(log, w_out, first, second, out, *copies):
    total = None
    for side, block in enumerate((first, second)):
        half = block.shape[1]
        part = contract_last(block[...], w_out[:, cols_of(0, side, half)])
        total = part if total is None else total + part
        copies[side][...] = block[...]
    out[...] = total


def last_kernel(items, w_out, *refs):
    blocks, (total, out, buf, sems) = refs[: len(items)], refs[len(items) :]
    pieces = sems.shape[0]
    step = total.shape[1] // pieces
    copies = []
    for k in range(pieces):
        rows = slice(k * step, (k + 1) * step)
        value = total[:, rows]
        for (mask, side), block in zip(items, blocks):
            value = value + contract_last(
                block[...], w_out[rows, cols_of(mask, side, block.shape[1])]
            )
        buf[:, rows] = value.astype(bf16)
        copies.append(pltpu.make_async_copy(buf.at[:, rows], out.at[:, rows], sems.at[k]))
        copies[-1].start()
    for copy in copies:
        copy.wait()


def local(n, context, w_out, residual, gain_temporal, w_in, gain_depth, w_depth, cotangent):
    frames, width = residual.shape
    half = width // 2
    share = frames // n
    features = width * n
    heads = w_out.shape[0]
    depth, act = w_depth.shape[1:]
    wide = depth // 2
    log = n.bit_length() - 1
    bits = [1 << i for i in range(log)]
    orders = (bits, bits[::-1])
    gain = gain_temporal[None, :]

    def swap(value, bit):
        return lax.ppermute(value, "mp", [(i, i ^ bit) for i in range(n)])

    def phase_of(mask, side):
        return min(i for i, bit in enumerate(orders[side]) if mask & bit)

    masks = sorted(range(1, n), key=lambda k: (-k.bit_count(), k))
    pairs = [((k, 0), (mirror(k, log), 1)) for k in masks]

    lists = [
        [[k for k in range(1, n) if phase_of(k, side) == i] for i in range(log)]
        for side in range(2)
    ]

    def share_items(phase, gots):
        items = []
        for side, order in enumerate(orders):
            masks = lists[side][phase] if phase < log else [0]
            items.append(
                [
                    (
                        k,
                        [
                            gots[j][1] + lists[side][j].index(k ^ order[j]) * share
                            for j in range(phase)
                        ],
                    )
                    for k in masks
                ]
            )
        return items, [value for values, _ in gots for value in values]

    def shares(phase, gots, after):
        items, listed = share_items(phase, gots)
        return list(
            call(
                functools.partial(shares_kernel, share, items),
                [((share * len(items[0]), wide), bf16)] * 2,
                [up] + listed,
                name="shares",
                after=after,
                cost=FREE,
            )
        )

    def both(values, i):
        return [swap(values[side], orders[side][i]) for side in range(2)]

    *values, up = call(
        functools.partial(upstream_kernel, share, [lists[side][0] for side in range(2)]),
        [((share * n // 2, wide), bf16)] * 2 + [((frames, depth), f32)],
        [cotangent[0], w_depth[0], gain_depth],
        [HBM] * 3,
        [
            pltpu.VMEM((frames, act), bf16),
            pltpu.VMEM((depth, act), bf16),
            pltpu.VMEM((1, depth), f32),
            pltpu.SemaphoreType.DMA((3,)),
        ],
        name="upstream",
    )
    share_gots = [(both(values, 0), 0)]

    arrived = {}
    token = up
    for pair in pairs:
        items, listed, riders, extra = [], [], None, 0
        for mask, side in pair:
            phase = phase_of(mask, side)
            listed += [arrived[mask ^ bit, side] for bit in orders[side][:phase]]
            items.append((mask, side, phase))
        if log == 2 and wide == half and pair is pairs[-2]:
            riders, more = share_items(1, share_gots)
            listed += [up] + more
            extra = share * len(riders[0])
        elif log != 2 and pair is pairs[-1]:
            for i in range(1, log):
                values = shares(i, share_gots, token)
                token = values[0]
                share_gots.append((both(values, i), 0))
        values = call(
            functools.partial(project_kernel, share, items, riders),
            [((frames + extra, half), bf16)] * 2,
            [context, w_out] + listed,
            name="project",
            after=token,
        )
        token = values[0]
        for (mask, side), value in zip(pair, values):
            arrived[mask, side] = swap(value, orders[side][phase_of(mask, side)])
        if riders:
            share_gots.append(([arrived[key] for key in pair[::-1]], frames))
    kept = call(
        keep_kernel,
        [((frames, width), f32)],
        [context, w_out, residual],
        name="keep",
        after=token,
    )[0]
    own_share = shares(log, share_gots, kept)
    share_got = both(own_share, 0)

    state, raw, squares, *sends = call(
        functools.partial(state_kernel, log),
        [((frames, width), f32), ((frames, depth), f32), ((SQ // 2, frames), f32)]
        + [((frames + SQ, wide), bf16), ((frames, wide), bf16)],
        [gain, w_in, kept] + [arrived[bit, side] for side in range(2) for bit in orders[side]],
        name="state",
        after=own_share[0],
    )
    haves = [[0], [0]]
    token = squares
    for i in range(log):
        got = both(sends, i)
        haves = [have + [k ^ orders[s][i] for k in have] for s, have in enumerate(haves)]
        if i < log - 1:
            own_share = list(
                call(
                    join_kernel,
                    [((2 * own_share[0].shape[0], wide), bf16)] * 2,
                    own_share + share_got,
                    name="join",
                    after=token,
                )
            )
            share_got = both(own_share, i + 1)
            raw, squares, *sends = call(
                reduce_kernel,
                [(raw.shape, f32), (squares.shape, f32)] + [((frames + SQ, wide), bf16), ((frames, wide), bf16)],
                [raw, squares] + got,
                name="reduce",
                after=own_share[0],
            )
            token = squares
    up_all = call(
        functools.partial(assemble_kernel, haves, share),
        [((frames, depth), bf16)],
        own_share + share_got,
        name="assemble",
        after=token,
    )[0]
    grads = call(
        functools.partial(back_kernel, features),
        [((frames, half), bf16)] * 2,
        [gain, w_in, up_all, state, raw, squares] + got,
        scratch=[pltpu.VMEM((frames, depth), bf16)],
        name="back",
    )

    total, *again = call(
        functools.partial(own_context_kernel, log),
        [((frames, heads), f32)] + [((frames, half), bf16)] * 2,
        [w_out] + list(grads),
        name="grad_context",
    )
    blocks = {(0, side): grads[side] for side in range(2)}
    for i in range(log):
        for k in range(1 << i):
            for side, order in enumerate(orders):
                mask = haves[side][k]
                value = again[side] if i and not k else blocks[mask, side]
                blocks[mask ^ order[i], side] = swap(value, order[i])

    depth_act, grad_residual = call(
        functools.partial(act_kernel, features),
        [((frames, act), bf16), ((frames, width), bf16)],
        [gain_depth, w_depth[0], raw, squares] + got + list(grads),
        scratch=[pltpu.VMEM((frames, depth), bf16)],
        name="act",
    )
    keys = [((haves[0][k], 0), (haves[1][k], 1)) for k in range(n)]
    for pair in keys[1:-1]:
        total = call(
            functools.partial(context_kernel, log, pair),
            [((frames, heads), f32)],
            [w_out] + [blocks[key] for key in pair] + [total],
            name="grad_context",
        )[0]
    grad_context = call(
        functools.partial(last_kernel, keys[-1]),
        [((frames, heads), bf16)],
        [w_out] + [blocks[key] for key in keys[-1]] + [total],
        scratch=[
            pltpu.VMEM((frames, heads), bf16),
            pltpu.SemaphoreType.DMA((min(OUT_PIECES, heads // LANES),)),
        ],
        name="grad_context",
        out_specs=[HBM],
    )[0]
    return (depth_act[None], grad_residual, grad_context)


def solution(mesh):
    in_specs = (
        P("dp", "mp"),
        P("mp", None),
        P("dp", "mp"),
        P(),
        P("mp", None),
        P("mp", None),
        P("mp", None, None),
        P("mp", "dp", None),
    )
    out_specs = (P("mp", "dp", None), P("dp", "mp"), P("dp", "mp"))
    n = mesh.shape["mp"]

    def run(*args):
        return local(n, *args)

    return jax.shard_map(run, mesh=mesh, in_specs=in_specs, out_specs=out_specs, check_vma=False)
```

```python
import functools

import jax
import jax.numpy as jnp
from jax import lax
from jax.experimental import pallas as pl
from jax.experimental.pallas import tpu as pltpu
from jax.sharding import PartitionSpec as P

EPS = 1e-05
LANES = 128
SQ = 16
OUT_PIECES = 4
bf16, f32 = jnp.bfloat16, jnp.float32
VMEM = pl.BlockSpec(memory_space=pltpu.VMEM)
HBM = pl.BlockSpec(memory_space=pltpu.HBM)

COST = pl.CostEstimate(flops=20 * 10**9, bytes_accessed=60 * 10**6, transcendentals=0)
FREE = pl.CostEstimate(flops=0, bytes_accessed=0, transcendentals=0)


def contract_last(left, right):
    return lax.dot_general(
        left, right, (((1,), (1,)), ((), ())), preferred_element_type=f32
    )


def mirror(mask, log):
    return sum(1 << (log - 1 - i) for i in range(log) if mask >> i & 1)


def call(body, outs, ins, in_specs=None, scratch=(), name=None, out_specs=None, after=None, cost=COST):
    in_specs = in_specs or [VMEM] * len(ins)
    ins = [
        pltpu.with_memory_space_constraint(a, pltpu.HBM) if spec is HBM else a
        for a, spec in zip(ins, in_specs)
    ]
    count = len(ins)
    kernel = body
    if after is not None:
        ins = ins + [after]
        in_specs = in_specs + [pl.BlockSpec(memory_space=pl.ANY)]

        def kernel(*refs):
            body(*refs[:count], *refs[count + 1 :])

    return pl.pallas_call(
        kernel,
        out_shape=[jax.ShapeDtypeStruct(s, d) for s, d in outs],
        in_specs=in_specs,
        out_specs=out_specs or [VMEM] * len(outs),
        scratch_shapes=list(scratch),
        compiler_params=pltpu.CompilerParams(vmem_limit_bytes=16 * 2**20),
        cost_estimate=cost,
        name=name,
    )(*ins)


def put_squares(out, at, squares):
    frames = squares.shape[1]
    high = squares.astype(bf16).astype(f32)
    both = jnp.concatenate([high, squares - high], axis=0).astype(bf16)
    out[at : at + SQ, :frames] = both
    if frames < out.shape[1]:
        out[at : at + SQ, frames:] = jnp.zeros((SQ, out.shape[1] - frames), bf16)


def get_squares(ref, at, frames):
    both = ref[at : at + SQ, :frames].astype(f32)
    return both[: SQ // 2] + both[SQ // 2 :]


def owner(mask):
    return lax.axis_index("mp") ^ mask


def span(start, size):
    return pl.ds(pl.multiple_of(start * size, size), size)


def cols_of(mask, side, half):
    return span(owner(mask) * 2 + side, half)


def upstream_kernel(share, masks, cot, w_depth, gain_hbm, *refs):
    *outs, up = refs[:-4]
    cot_buf, depth_buf, gain_depth, sems = refs[-4:]
    pieces = sems.shape[0] - 2
    step = depth_buf.shape[0] // pieces
    pairs = [(cot, cot_buf), (gain_hbm, gain_depth)]
    for k in range(pieces):
        rows = pl.ds(k * step, step)
        pairs.append((w_depth.at[rows, :], depth_buf.at[rows, :]))
    copies = [pltpu.make_async_copy(a, b, sems.at[i]) for i, (a, b) in enumerate(pairs)]
    for copy in copies:
        copy.start()
    copies[0].wait()
    copies[1].wait()
    for k in range(pieces):
        copies[2 + k].wait()
        cols = slice(k * step, (k + 1) * step)
        up[:, cols] = gain_depth[:, cols] * contract_last(cot_buf[...], depth_buf[cols, :])
    wide = up.shape[1] // 2
    for side, out in enumerate(outs):
        for i, mask in enumerate(masks[side]):
            out[i * share : (i + 1) * share, :] = up[
                span(owner(mask), share), side * wide : (side + 1) * wide
            ].astype(bf16)


def put_shares(share, items, up, gots, outs, first):
    wide = up.shape[1] // 2
    for side, (rows, out) in enumerate(zip(items, outs)):
        for i, (mask, places) in enumerate(rows):
            part = up[span(owner(mask), share), side * wide : (side + 1) * wide]
            for phase, at in enumerate(places):
                part = part + gots[2 * phase + side][at : at + share, :].astype(f32)
            out[first + i * share : first + (i + 1) * share, :] = part.astype(bf16)


def shares_kernel(share, items, up, *refs):
    put_shares(share, items, up, refs[:-2], refs[-2:], 0)


def join_kernel(*refs):
    for side in range(2):
        first, second, out = refs[side], refs[2 + side], refs[4 + side]
        out[: first.shape[0], :] = first[...]
        out[first.shape[0] :, :] = second[...]


def project_kernel(share, items, riders, context, w_out, *refs):
    adds, outs = refs[: -len(items)], refs[-len(items) :]
    half = outs[0].shape[1]
    frames = context.shape[0]
    at = 0
    for (mask, side, count), out in zip(items, outs):
        product = jnp.dot(
            context[...], w_out[:, cols_of(mask, side, half)], preferred_element_type=f32
        )
        for add in adds[at : at + count]:
            product = product + add[:frames, :].astype(f32)
        out[:frames, :] = product.astype(bf16)
        at += count
    if riders:
        put_shares(share, riders, adds[at], adds[at + 1 :], outs[::-1], frames)


def product_kernel(items, context, w_out, *outs):
    for (mask, side), out in zip(items, outs):
        out[...] = jnp.dot(
            context[...],
            w_out[:, cols_of(mask, side, out.shape[1])],
            preferred_element_type=f32,
        )


def add_kernel(counts, *refs):
    products, adds, outs = refs[:2], refs[2:-2], refs[-2:]
    at = 0
    for product, count, out in zip(products, counts, outs):
        total = product[...]
        for add in adds[at : at + count]:
            total = total + add[: total.shape[0], :].astype(f32)
        out[...] = total.astype(bf16)
        at += count


def keep_kernel(context, w_out, residual, out):
    out[...] = residual[...].astype(f32) + jnp.dot(
        context[...],
        w_out[:, span(lax.axis_index("mp"), out.shape[1])],
        preferred_element_type=f32,
    )


def state_kernel(log, gain, w_in, kept, *refs):
    adds, (state, raw, squares, *sends) = refs[: 2 * log], refs[2 * log :]
    frames, width = state.shape
    half = width // 2
    wide = raw.shape[1] // 2
    for side in range(2):
        cols = slice(side * half, (side + 1) * half)
        total = kept[:, cols]
        for add in adds[side * log : (side + 1) * log]:
            total = total + add[:frames, :].astype(f32)
        state[:, cols] = total
    value = state[...]
    gains = gain[:, span(lax.axis_index("mp"), width)]
    raw[...] = jnp.dot((value * gains).astype(bf16), w_in[...], preferred_element_type=f32)
    column = jnp.sum(value * value, axis=1, keepdims=True)
    row = jnp.transpose(jnp.broadcast_to(column, (frames, LANES)))[: SQ // 2]
    for side, send in enumerate(sends):
        send[:frames, :] = raw[:, side * wide : (side + 1) * wide].astype(bf16)
    squares[...] = row
    put_squares(sends[0], frames, row)


def reduce_kernel(raw, squares, *refs):
    got, (raw_out, squares_out, *sends) = refs[:2], refs[2:]
    frames, depth = raw.shape
    wide = depth // 2
    for side in range(2):
        cols = slice(side * wide, (side + 1) * wide)
        total = raw[:, cols] + got[side][:frames, :].astype(f32)
        raw_out[:, cols] = total
        sends[side][:frames, :] = total.astype(bf16)
    row = squares[...] + get_squares(got[0], frames, frames)
    squares_out[...] = row
    put_squares(sends[0], frames, row)


def depth_rows(raw, got, rows):
    wide = raw.shape[1] // 2
    return jnp.concatenate(
        [
            raw[rows, side * wide : (side + 1) * wide] + got[side][rows, :].astype(f32)
            for side in range(2)
        ],
        axis=1,
    )


def recip_of(squares, got, frames, features):
    row = squares[...] + get_squares(got[0], frames, frames)
    return jnp.transpose(
        jnp.broadcast_to(lax.rsqrt(row[:1] / features + EPS), (LANES, frames))
    )[:, :1]


def assemble_kernel(haves, share, *refs):
    sent, rest, up = refs[:2], refs[2:4], refs[4]
    wide = up.shape[1] // 2
    for side in range(2):
        held = sent[side].shape[0]
        for i, mask in enumerate(haves[side]):
            at = i * share
            ref, at = (sent[side], at) if at < held else (rest[side], at - held)
            up[span(owner(mask), share), side * wide : (side + 1) * wide] = ref[
                at : at + share, :
            ]


def back_kernel(features, gain, w_in, up, state, raw, squares, *refs):
    got, (*grads, du) = refs[:2], refs[2:]
    frames, width = state.shape
    half = width // 2
    recip = recip_of(squares, got, frames, features)
    back = []
    step = 64 if frames % 64 == 0 else frames
    for at in range(0, frames, step):
        rows = slice(at, at + step)
        depth_in = depth_rows(raw, got, rows) * recip[rows]
        upstream = up[rows, :].astype(f32)
        urecip = lax.rsqrt(jnp.mean(depth_in * depth_in, axis=1, keepdims=True) + EPS)
        inner = jnp.mean(depth_in * upstream, axis=1, keepdims=True)
        part = urecip * upstream - depth_in * (urecip * urecip * urecip * inner)
        part = part.astype(bf16)
        du[rows, :] = part
        dot_du = jnp.sum(part.astype(f32) * depth_in, axis=1, keepdims=True) / recip[rows]
        back.append(recip[rows] * recip[rows] * recip[rows] * (dot_du / features))
    back = jnp.concatenate(back, axis=0)
    gains = gain[:, span(lax.axis_index("mp"), width)]
    for side, grad in enumerate(grads):
        cols = slice(side * half, (side + 1) * half)
        dnormed = contract_last(du[...], w_in[cols, :])
        grad[...] = (recip * (gains[:, cols] * dnormed) - state[:, cols] * back).astype(bf16)


def act_kernel(features, gain_depth, w_depth, raw, squares, *refs):
    got, grads, (out, grad_out, latent) = refs[:2], refs[2:4], refs[4:]
    frames = raw.shape[0]
    half = grads[0].shape[1]
    for side in range(2):
        grad_out[:, side * half : (side + 1) * half] = grads[side][...]
    recip = recip_of(squares, got, frames, features)
    step = 64 if frames % 64 == 0 else frames
    for at in range(0, frames, step):
        rows = slice(at, at + step)
        depth_in = depth_rows(raw, got, rows) * recip[rows]
        urecip = lax.rsqrt(jnp.mean(depth_in * depth_in, axis=1, keepdims=True) + EPS)
        latent[rows, :] = (depth_in * urecip * gain_depth[...]).astype(bf16)
    out[...] = jnp.dot(latent[...], w_depth[...], preferred_element_type=f32).astype(bf16)


def context_kernel(log, items, w_out, *refs):
    blocks, rest, out = refs[: len(items)], refs[len(items) : -1], refs[-1]
    total = rest[0][...]
    for (mask, side), block in zip(items, blocks):
        part = contract_last(block[...], w_out[:, cols_of(mask, side, block.shape[1])])
        total = total + part
    out[...] = total


def own_context_kernel(log, w_out, first, second, out, *copies):
    total = None
    for side, block in enumerate((first, second)):
        half = block.shape[1]
        part = contract_last(block[...], w_out[:, cols_of(0, side, half)])
        total = part if total is None else total + part
        copies[side][...] = block[...]
    out[...] = total


def last_kernel(items, w_out, *refs):
    blocks, (total, out, buf, sems) = refs[: len(items)], refs[len(items) :]
    pieces = sems.shape[0]
    step = total.shape[1] // pieces
    copies = []
    for k in range(pieces):
        rows = slice(k * step, (k + 1) * step)
        value = total[:, rows]
        for (mask, side), block in zip(items, blocks):
            value = value + contract_last(
                block[...], w_out[rows, cols_of(mask, side, block.shape[1])]
            )
        buf[:, rows] = value.astype(bf16)
        copies.append(pltpu.make_async_copy(buf.at[:, rows], out.at[:, rows], sems.at[k]))
        copies[-1].start()
    for copy in copies:
        copy.wait()


def local(n, context, w_out, residual, gain_temporal, w_in, gain_depth, w_depth, cotangent):
    frames, width = residual.shape
    half = width // 2
    share = frames // n
    features = width * n
    heads = w_out.shape[0]
    depth, act = w_depth.shape[1:]
    wide = depth // 2
    log = n.bit_length() - 1
    bits = [1 << i for i in range(log)]
    orders = (bits, bits[::-1])
    gain = gain_temporal[None, :]

    def swap(value, bit):
        return lax.ppermute(value, "mp", [(i, i ^ bit) for i in range(n)])

    def phase_of(mask, side):
        return min(i for i, bit in enumerate(orders[side]) if mask & bit)

    masks = sorted(range(1, n), key=lambda k: (-k.bit_count(), k))
    pairs = [((k, 0), (mirror(k, log), 1)) for k in masks]

    lists = [
        [[k for k in range(1, n) if phase_of(k, side) == i] for i in range(log)]
        for side in range(2)
    ]

    def share_items(phase, gots):
        items = []
        for side, order in enumerate(orders):
            masks = lists[side][phase] if phase < log else [0]
            items.append(
                [
                    (
                        k,
                        [
                            gots[j][1] + lists[side][j].index(k ^ order[j]) * share
                            for j in range(phase)
                        ],
                    )
                    for k in masks
                ]
            )
        return items, [value for values, _ in gots for value in values]

    def shares(phase, gots, after):
        items, listed = share_items(phase, gots)
        return list(
            call(
                functools.partial(shares_kernel, share, items),
                [((share * len(items[0]), wide), bf16)] * 2,
                [up] + listed,
                name="shares",
                after=after,
                cost=FREE,
            )
        )

    def both(values, i):
        return [swap(values[side], orders[side][i]) for side in range(2)]

    *values, up = call(
        functools.partial(upstream_kernel, share, [lists[side][0] for side in range(2)]),
        [((share * n // 2, wide), bf16)] * 2 + [((frames, depth), f32)],
        [cotangent[0], w_depth[0], gain_depth],
        [HBM] * 3,
        [
            pltpu.VMEM((frames, act), bf16),
            pltpu.VMEM((depth, act), bf16),
            pltpu.VMEM((1, depth), f32),
            pltpu.SemaphoreType.DMA((3,)),
        ],
        name="upstream",
    )
    share_gots = [(both(values, 0), 0)]

    arrived = {}
    token = up
    for pair in pairs:
        items, listed, riders, extra = [], [], None, 0
        for mask, side in pair:
            phase = phase_of(mask, side)
            listed += [arrived[mask ^ bit, side] for bit in orders[side][:phase]]
            items.append((mask, side, phase))
        if log == 2 and wide == half and pair is pairs[-2]:
            riders, more = share_items(1, share_gots)
            listed += [up] + more
            extra = share * len(riders[0])
        elif log != 2 and pair is pairs[-1]:
            for i in range(1, log):
                values = shares(i, share_gots, token)
                token = values[0]
                share_gots.append((both(values, i), 0))
        if pair is pairs[-1]:
            products = call(
                functools.partial(product_kernel, pair),
                [((frames, half), f32)] * 2,
                [context, w_out],
                name="product",
                after=token,
            )
            values = call(
                functools.partial(add_kernel, [count for _, _, count in items]),
                [((frames, half), bf16)] * 2,
                list(products) + listed,
                name="add",
                cost=FREE,
                after=token,
            )
        else:
            values = call(
                functools.partial(project_kernel, share, items, riders),
                [((frames + extra, half), bf16)] * 2,
                [context, w_out] + listed,
                name="project",
                after=token,
            )
        token = values[0]
        for (mask, side), value in zip(pair, values):
            arrived[mask, side] = swap(value, orders[side][phase_of(mask, side)])
        if riders:
            share_gots.append(([arrived[key] for key in pair[::-1]], frames))
    kept = call(
        keep_kernel,
        [((frames, width), f32)],
        [context, w_out, residual],
        name="keep",
        cost=FREE,
        after=token,
    )[0]
    own_share = shares(log, share_gots, kept)
    share_got = both(own_share, 0)

    state, raw, squares, *sends = call(
        functools.partial(state_kernel, log),
        [((frames, width), f32), ((frames, depth), f32), ((SQ // 2, frames), f32)]
        + [((frames + SQ, wide), bf16), ((frames, wide), bf16)],
        [gain, w_in, kept] + [arrived[bit, side] for side in range(2) for bit in orders[side]],
        name="state",
        after=own_share[0],
    )
    haves = [[0], [0]]
    token = squares
    for i in range(log):
        got = both(sends, i)
        haves = [have + [k ^ orders[s][i] for k in have] for s, have in enumerate(haves)]
        if i < log - 1:
            own_share = list(
                call(
                    join_kernel,
                    [((2 * own_share[0].shape[0], wide), bf16)] * 2,
                    own_share + share_got,
                    name="join",
                    after=token,
                )
            )
            share_got = both(own_share, i + 1)
            raw, squares, *sends = call(
                reduce_kernel,
                [(raw.shape, f32), (squares.shape, f32)] + [((frames + SQ, wide), bf16), ((frames, wide), bf16)],
                [raw, squares] + got,
                name="reduce",
                after=own_share[0],
            )
            token = squares
    up_all = call(
        functools.partial(assemble_kernel, haves, share),
        [((frames, depth), bf16)],
        own_share + share_got,
        name="assemble",
        after=token,
    )[0]
    grads = call(
        functools.partial(back_kernel, features),
        [((frames, half), bf16)] * 2,
        [gain, w_in, up_all, state, raw, squares] + got,
        scratch=[pltpu.VMEM((frames, depth), bf16)],
        name="back",
    )

    total, *again = call(
        functools.partial(own_context_kernel, log),
        [((frames, heads), f32)] + [((frames, half), bf16)] * 2,
        [w_out] + list(grads),
        name="grad_context",
    )
    blocks = {(0, side): grads[side] for side in range(2)}
    for i in range(log):
        for k in range(1 << i):
            for side, order in enumerate(orders):
                mask = haves[side][k]
                value = again[side] if i and not k else blocks[mask, side]
                blocks[mask ^ order[i], side] = swap(value, order[i])

    depth_act, grad_residual = call(
        functools.partial(act_kernel, features),
        [((frames, act), bf16), ((frames, width), bf16)],
        [gain_depth, w_depth[0], raw, squares] + got + list(grads),
        scratch=[pltpu.VMEM((frames, depth), bf16)],
        name="act",
    )
    keys = [((haves[0][k], 0), (haves[1][k], 1)) for k in range(n)]
    for pair in keys[1:-1]:
        total = call(
            functools.partial(context_kernel, log, pair),
            [((frames, heads), f32)],
            [w_out] + [blocks[key] for key in pair] + [total],
            name="grad_context",
        )[0]
    grad_context = call(
        functools.partial(last_kernel, keys[-1]),
        [((frames, heads), bf16)],
        [w_out] + [blocks[key] for key in keys[-1]] + [total],
        scratch=[
            pltpu.VMEM((frames, heads), bf16),
            pltpu.SemaphoreType.DMA((min(OUT_PIECES, heads // LANES),)),
        ],
        name="grad_context",
        out_specs=[HBM],
    )[0]
    return (depth_act[None], grad_residual, grad_context)


def solution(mesh):
    in_specs = (
        P("dp", "mp"),
        P("mp", None),
        P("dp", "mp"),
        P(),
        P("mp", None),
        P("mp", None),
        P("mp", None, None),
        P("mp", "dp", None),
    )
    out_specs = (P("mp", "dp", None), P("dp", "mp"), P("dp", "mp"))
    n = mesh.shape["mp"]

    def run(*args):
        return local(n, *args)

    return jax.shard_map(run, mesh=mesh, in_specs=in_specs, out_specs=out_specs, check_vma=False)
```

```python
import functools

import jax
import jax.numpy as jnp
from jax import lax
from jax.experimental import pallas as pl
from jax.experimental.pallas import tpu as pltpu
from jax.sharding import PartitionSpec as P

EPS = 1e-05
LANES = 128
SQ = 16
OUT_PIECES = 4
bf16, f32 = jnp.bfloat16, jnp.float32
VMEM = pl.BlockSpec(memory_space=pltpu.VMEM)
HBM = pl.BlockSpec(memory_space=pltpu.HBM)

COST = pl.CostEstimate(flops=20 * 10**9, bytes_accessed=60 * 10**6, transcendentals=0)
FREE = pl.CostEstimate(flops=0, bytes_accessed=0, transcendentals=0)


def contract_last(left, right):
    return lax.dot_general(
        left, right, (((1,), (1,)), ((), ())), preferred_element_type=f32
    )


def mirror(mask, log):
    return sum(1 << (log - 1 - i) for i in range(log) if mask >> i & 1)


def call(body, outs, ins, in_specs=None, scratch=(), name=None, out_specs=None, after=None, cost=COST):
    in_specs = in_specs or [VMEM] * len(ins)
    ins = [
        pltpu.with_memory_space_constraint(a, pltpu.HBM) if spec is HBM else a
        for a, spec in zip(ins, in_specs)
    ]
    count = len(ins)
    kernel = body
    if after is not None:
        ins = ins + [after]
        in_specs = in_specs + [pl.BlockSpec(memory_space=pl.ANY)]

        def kernel(*refs):
            body(*refs[:count], *refs[count + 1 :])

    return pl.pallas_call(
        kernel,
        out_shape=[jax.ShapeDtypeStruct(s, d) for s, d in outs],
        in_specs=in_specs,
        out_specs=out_specs or [VMEM] * len(outs),
        scratch_shapes=list(scratch),
        compiler_params=pltpu.CompilerParams(vmem_limit_bytes=16 * 2**20),
        cost_estimate=cost,
        name=name,
    )(*ins)


def put_squares(out, at, squares):
    frames = squares.shape[1]
    high = squares.astype(bf16).astype(f32)
    both = jnp.concatenate([high, squares - high], axis=0).astype(bf16)
    out[at : at + SQ, :frames] = both
    if frames < out.shape[1]:
        out[at : at + SQ, frames:] = jnp.zeros((SQ, out.shape[1] - frames), bf16)


def get_squares(ref, at, frames):
    both = ref[at : at + SQ, :frames].astype(f32)
    return both[: SQ // 2] + both[SQ // 2 :]


def owner(mask):
    return lax.axis_index("mp") ^ mask


def span(start, size):
    return pl.ds(pl.multiple_of(start * size, size), size)


def cols_of(mask, side, half):
    return span(owner(mask) * 2 + side, half)


def upstream_kernel(share, masks, cot, w_depth, gain_hbm, *refs):
    *outs, up = refs[:-4]
    cot_buf, depth_buf, gain_depth, sems = refs[-4:]
    pieces = sems.shape[0] - 2
    step = depth_buf.shape[0] // pieces
    pairs = [(cot, cot_buf), (gain_hbm, gain_depth)]
    for k in range(pieces):
        rows = pl.ds(k * step, step)
        pairs.append((w_depth.at[rows, :], depth_buf.at[rows, :]))
    copies = [pltpu.make_async_copy(a, b, sems.at[i]) for i, (a, b) in enumerate(pairs)]
    for copy in copies:
        copy.start()
    copies[0].wait()
    copies[1].wait()
    for k in range(pieces):
        copies[2 + k].wait()
        cols = slice(k * step, (k + 1) * step)
        up[:, cols] = gain_depth[:, cols] * contract_last(cot_buf[...], depth_buf[cols, :])
    wide = up.shape[1] // 2
    for side, out in enumerate(outs):
        for i, mask in enumerate(masks[side]):
            out[i * share : (i + 1) * share, :] = up[
                span(owner(mask), share), side * wide : (side + 1) * wide
            ].astype(bf16)


def put_shares(share, items, up, gots, outs, first):
    wide = up.shape[1] // 2
    for side, (rows, out) in enumerate(zip(items, outs)):
        for i, (mask, places) in enumerate(rows):
            part = up[span(owner(mask), share), side * wide : (side + 1) * wide]
            for phase, at in enumerate(places):
                part = part + gots[2 * phase + side][at : at + share, :].astype(f32)
            out[first + i * share : first + (i + 1) * share, :] = part.astype(bf16)


def shares_kernel(share, items, up, *refs):
    put_shares(share, items, up, refs[:-2], refs[-2:], 0)


def join_kernel(*refs):
    for side in range(2):
        first, second, out = refs[side], refs[2 + side], refs[4 + side]
        out[: first.shape[0], :] = first[...]
        out[first.shape[0] :, :] = second[...]


def project_kernel(share, items, riders, context, w_out, *refs):
    adds, outs = refs[: -len(items)], refs[-len(items) :]
    half = outs[0].shape[1]
    frames = context.shape[0]
    at = 0
    for (mask, side, count), out in zip(items, outs):
        product = jnp.dot(
            context[...], w_out[:, cols_of(mask, side, half)], preferred_element_type=f32
        )
        for add in adds[at : at + count]:
            product = product + add[:frames, :].astype(f32)
        out[:frames, :] = product.astype(bf16)
        at += count
    if riders:
        put_shares(share, riders, adds[at], adds[at + 1 :], outs[::-1], frames)


def keep_kernel(context, w_out, residual, out):
    out[...] = residual[...].astype(f32) + jnp.dot(
        context[...],
        w_out[:, span(lax.axis_index("mp"), out.shape[1])],
        preferred_element_type=f32,
    )


def state_kernel(log, gain, w_in, kept, *refs):
    adds, (state, raw, squares, *sends) = refs[: 2 * log], refs[2 * log :]
    frames, width = state.shape
    half = width // 2
    wide = raw.shape[1] // 2
    for side in range(2):
        cols = slice(side * half, (side + 1) * half)
        total = kept[:, cols]
        for add in adds[side * log : (side + 1) * log]:
            total = total + add[:frames, :].astype(f32)
        state[:, cols] = total
    value = state[...]
    gains = gain[:, span(lax.axis_index("mp"), width)]
    raw[...] = jnp.dot((value * gains).astype(bf16), w_in[...], preferred_element_type=f32)
    column = jnp.sum(value * value, axis=1, keepdims=True)
    row = jnp.transpose(jnp.broadcast_to(column, (frames, LANES)))[: SQ // 2]
    for side, send in enumerate(sends):
        send[:frames, :] = raw[:, side * wide : (side + 1) * wide].astype(bf16)
    squares[...] = row
    put_squares(sends[0], frames, row)


def reduce_kernel(raw, squares, *refs):
    got, (raw_out, squares_out, *sends) = refs[:2], refs[2:]
    frames, depth = raw.shape
    wide = depth // 2
    for side in range(2):
        cols = slice(side * wide, (side + 1) * wide)
        total = raw[:, cols] + got[side][:frames, :].astype(f32)
        raw_out[:, cols] = total
        sends[side][:frames, :] = total.astype(bf16)
    row = squares[...] + get_squares(got[0], frames, frames)
    squares_out[...] = row
    put_squares(sends[0], frames, row)


def depth_rows(raw, got, rows):
    wide = raw.shape[1] // 2
    return jnp.concatenate(
        [
            raw[rows, side * wide : (side + 1) * wide] + got[side][rows, :].astype(f32)
            for side in range(2)
        ],
        axis=1,
    )


def recip_of(squares, got, frames, features):
    row = squares[...] + get_squares(got[0], frames, frames)
    return jnp.transpose(
        jnp.broadcast_to(lax.rsqrt(row[:1] / features + EPS), (LANES, frames))
    )[:, :1]


def assemble_kernel(haves, share, *refs):
    sent, rest, up = refs[:2], refs[2:4], refs[4]
    wide = up.shape[1] // 2
    for side in range(2):
        held = sent[side].shape[0]
        for i, mask in enumerate(haves[side]):
            at = i * share
            ref, at = (sent[side], at) if at < held else (rest[side], at - held)
            up[span(owner(mask), share), side * wide : (side + 1) * wide] = ref[
                at : at + share, :
            ]


def back_kernel(features, gain, w_in, up, state, raw, squares, *refs):
    got, (*grads, du) = refs[:2], refs[2:]
    frames, width = state.shape
    half = width // 2
    recip = recip_of(squares, got, frames, features)
    back = []
    step = 64 if frames % 64 == 0 else frames
    for at in range(0, frames, step):
        rows = slice(at, at + step)
        depth_in = depth_rows(raw, got, rows) * recip[rows]
        upstream = up[rows, :].astype(f32)
        urecip = lax.rsqrt(jnp.mean(depth_in * depth_in, axis=1, keepdims=True) + EPS)
        inner = jnp.mean(depth_in * upstream, axis=1, keepdims=True)
        part = urecip * upstream - depth_in * (urecip * urecip * urecip * inner)
        part = part.astype(bf16)
        du[rows, :] = part
        dot_du = jnp.sum(part.astype(f32) * depth_in, axis=1, keepdims=True)
        back.append(recip[rows] * recip[rows] * (dot_du * (1.0 / features)))
    back = jnp.concatenate(back, axis=0)
    gains = gain[:, span(lax.axis_index("mp"), width)]
    for side, grad in enumerate(grads):
        cols = slice(side * half, (side + 1) * half)
        dnormed = contract_last(du[...], w_in[cols, :])
        grad[...] = (recip * (gains[:, cols] * dnormed) - state[:, cols] * back).astype(bf16)


def act_kernel(features, gain_depth, w_depth, raw, squares, *refs):
    got, grads, (out, grad_out, latent) = refs[:2], refs[2:4], refs[4:]
    frames = raw.shape[0]
    half = grads[0].shape[1]
    for side in range(2):
        grad_out[:, side * half : (side + 1) * half] = grads[side][...]
    recip = recip_of(squares, got, frames, features)
    step = 64 if frames % 64 == 0 else frames
    for at in range(0, frames, step):
        rows = slice(at, at + step)
        depth_in = depth_rows(raw, got, rows) * recip[rows]
        urecip = lax.rsqrt(jnp.mean(depth_in * depth_in, axis=1, keepdims=True) + EPS)
        latent[rows, :] = (depth_in * urecip * gain_depth[...]).astype(bf16)
    out[...] = jnp.dot(latent[...], w_depth[...], preferred_element_type=f32).astype(bf16)


def context_kernel(log, items, w_out, *refs):
    blocks, rest, out = refs[: len(items)], refs[len(items) : -1], refs[-1]
    total = rest[0][...]
    for (mask, side), block in zip(items, blocks):
        part = contract_last(block[...], w_out[:, cols_of(mask, side, block.shape[1])])
        total = total + part
    out[...] = total


def own_context_kernel(log, w_out, first, second, out, *copies):
    total = None
    for side, block in enumerate((first, second)):
        half = block.shape[1]
        part = contract_last(block[...], w_out[:, cols_of(0, side, half)])
        total = part if total is None else total + part
        copies[side][...] = block[...]
    out[...] = total


def last_kernel(items, w_out, *refs):
    blocks, (total, out, buf, sems) = refs[: len(items)], refs[len(items) :]
    pieces = sems.shape[0]
    step = total.shape[1] // pieces
    copies = []
    for k in range(pieces):
        rows = slice(k * step, (k + 1) * step)
        value = total[:, rows]
        for (mask, side), block in zip(items, blocks):
            value = value + contract_last(
                block[...], w_out[rows, cols_of(mask, side, block.shape[1])]
            )
        buf[:, rows] = value.astype(bf16)
        copies.append(pltpu.make_async_copy(buf.at[:, rows], out.at[:, rows], sems.at[k]))
        copies[-1].start()
    for copy in copies:
        copy.wait()


def local(n, context, w_out, residual, gain_temporal, w_in, gain_depth, w_depth, cotangent):
    frames, width = residual.shape
    half = width // 2
    share = frames // n
    features = width * n
    heads = w_out.shape[0]
    depth, act = w_depth.shape[1:]
    wide = depth // 2
    log = n.bit_length() - 1
    bits = [1 << i for i in range(log)]
    orders = (bits, bits[::-1])
    gain = gain_temporal[None, :]

    def swap(value, bit):
        return lax.ppermute(value, "mp", [(i, i ^ bit) for i in range(n)])

    def phase_of(mask, side):
        return min(i for i, bit in enumerate(orders[side]) if mask & bit)

    masks = sorted(range(1, n), key=lambda k: (-k.bit_count(), k))
    pairs = [((k, 0), (mirror(k, log), 1)) for k in masks]

    lists = [
        [[k for k in range(1, n) if phase_of(k, side) == i] for i in range(log)]
        for side in range(2)
    ]

    def share_items(phase, gots):
        items = []
        for side, order in enumerate(orders):
            masks = lists[side][phase] if phase < log else [0]
            items.append(
                [
                    (
                        k,
                        [
                            gots[j][1] + lists[side][j].index(k ^ order[j]) * share
                            for j in range(phase)
                        ],
                    )
                    for k in masks
                ]
            )
        return items, [value for values, _ in gots for value in values]

    def shares(phase, gots, after):
        items, listed = share_items(phase, gots)
        return list(
            call(
                functools.partial(shares_kernel, share, items),
                [((share * len(items[0]), wide), bf16)] * 2,
                [up] + listed,
                name="shares",
                after=after,
                cost=FREE,
            )
        )

    def both(values, i):
        return [swap(values[side], orders[side][i]) for side in range(2)]

    *values, up = call(
        functools.partial(upstream_kernel, share, [lists[side][0] for side in range(2)]),
        [((share * n // 2, wide), bf16)] * 2 + [((frames, depth), f32)],
        [cotangent[0], w_depth[0], gain_depth],
        [HBM] * 3,
        [
            pltpu.VMEM((frames, act), bf16),
            pltpu.VMEM((depth, act), bf16),
            pltpu.VMEM((1, depth), f32),
            pltpu.SemaphoreType.DMA((3,)),
        ],
        name="upstream",
    )
    share_gots = [(both(values, 0), 0)]

    arrived = {}
    token = up
    for pair in pairs:
        items, listed, riders, extra = [], [], None, 0
        for mask, side in pair:
            phase = phase_of(mask, side)
            listed += [arrived[mask ^ bit, side] for bit in orders[side][:phase]]
            items.append((mask, side, phase))
        if log == 2 and wide == half and pair is pairs[-2]:
            riders, more = share_items(1, share_gots)
            listed += [up] + more
            extra = share * len(riders[0])
        elif log != 2 and pair is pairs[-1]:
            for i in range(1, log):
                values = shares(i, share_gots, token)
                token = values[0]
                share_gots.append((both(values, i), 0))
        values = call(
            functools.partial(project_kernel, share, items, riders),
            [((frames + extra, half), bf16)] * 2,
            [context, w_out] + listed,
            name="project",
            after=token,
        )
        token = values[0]
        for (mask, side), value in zip(pair, values):
            arrived[mask, side] = swap(value, orders[side][phase_of(mask, side)])
        if riders:
            share_gots.append(([arrived[key] for key in pair[::-1]], frames))
    kept = call(
        keep_kernel,
        [((frames, width), f32)],
        [context, w_out, residual],
        name="keep",
        after=token,
    )[0]
    own_share = shares(log, share_gots, kept)
    share_got = both(own_share, 0)

    state, raw, squares, *sends = call(
        functools.partial(state_kernel, log),
        [((frames, width), f32), ((frames, depth), f32), ((SQ // 2, frames), f32)]
        + [((frames + SQ, wide), bf16), ((frames, wide), bf16)],
        [gain, w_in, kept] + [arrived[bit, side] for side in range(2) for bit in orders[side]],
        name="state",
        after=own_share[0],
    )
    haves = [[0], [0]]
    token = squares
    for i in range(log):
        got = both(sends, i)
        haves = [have + [k ^ orders[s][i] for k in have] for s, have in enumerate(haves)]
        if i < log - 1:
            own_share = list(
                call(
                    join_kernel,
                    [((2 * own_share[0].shape[0], wide), bf16)] * 2,
                    own_share + share_got,
                    name="join",
                    after=token,
                )
            )
            share_got = both(own_share, i + 1)
            raw, squares, *sends = call(
                reduce_kernel,
                [(raw.shape, f32), (squares.shape, f32)] + [((frames + SQ, wide), bf16), ((frames, wide), bf16)],
                [raw, squares] + got,
                name="reduce",
                after=own_share[0],
            )
            token = squares
    up_all = call(
        functools.partial(assemble_kernel, haves, share),
        [((frames, depth), bf16)],
        own_share + share_got,
        name="assemble",
        after=token,
    )[0]
    grads = call(
        functools.partial(back_kernel, features),
        [((frames, half), bf16)] * 2,
        [gain, w_in, up_all, state, raw, squares] + got,
        scratch=[pltpu.VMEM((frames, depth), bf16)],
        name="back",
    )

    total, *again = call(
        functools.partial(own_context_kernel, log),
        [((frames, heads), f32)] + [((frames, half), bf16)] * 2,
        [w_out] + list(grads),
        name="grad_context",
    )
    blocks = {(0, side): grads[side] for side in range(2)}
    for i in range(log):
        for k in range(1 << i):
            for side, order in enumerate(orders):
                mask = haves[side][k]
                value = again[side] if i and not k else blocks[mask, side]
                blocks[mask ^ order[i], side] = swap(value, order[i])

    depth_act, grad_residual = call(
        functools.partial(act_kernel, features),
        [((frames, act), bf16), ((frames, width), bf16)],
        [gain_depth, w_depth[0], raw, squares] + got + list(grads),
        scratch=[pltpu.VMEM((frames, depth), bf16)],
        name="act",
    )
    keys = [((haves[0][k], 0), (haves[1][k], 1)) for k in range(n)]
    for pair in keys[1:-1]:
        total = call(
            functools.partial(context_kernel, log, pair),
            [((frames, heads), f32)],
            [w_out] + [blocks[key] for key in pair] + [total],
            name="grad_context",
        )[0]
    grad_context = call(
        functools.partial(last_kernel, keys[-1]),
        [((frames, heads), bf16)],
        [w_out] + [blocks[key] for key in keys[-1]] + [total],
        scratch=[
            pltpu.VMEM((frames, heads), bf16),
            pltpu.SemaphoreType.DMA((min(OUT_PIECES, heads // LANES),)),
        ],
        name="grad_context",
        out_specs=[HBM],
    )[0]
    return (depth_act[None], grad_residual, grad_context)


def solution(mesh):
    in_specs = (
        P("dp", "mp"),
        P("mp", None),
        P("dp", "mp"),
        P(),
        P("mp", None),
        P("mp", None),
        P("mp", None, None),
        P("mp", "dp", None),
    )
    out_specs = (P("mp", "dp", None), P("dp", "mp"), P("dp", "mp"))
    n = mesh.shape["mp"]

    def run(*args):
        return local(n, *args)

    return jax.shard_map(run, mesh=mesh, in_specs=in_specs, out_specs=out_specs, check_vma=False)
```

```python
import functools

import jax
import jax.numpy as jnp
from jax import lax
from jax.experimental import pallas as pl
from jax.experimental.pallas import tpu as pltpu
from jax.sharding import PartitionSpec as P

EPS = 1e-05
LANES = 128
SQ = 16
OUT_PIECES = 4
bf16, f32 = jnp.bfloat16, jnp.float32
VMEM = pl.BlockSpec(memory_space=pltpu.VMEM)
HBM = pl.BlockSpec(memory_space=pltpu.HBM)

COST = pl.CostEstimate(flops=20 * 10**9, bytes_accessed=60 * 10**6, transcendentals=0)
FREE = pl.CostEstimate(flops=0, bytes_accessed=0, transcendentals=0)


def contract_last(left, right):
    return lax.dot_general(
        left, right, (((1,), (1,)), ((), ())), preferred_element_type=f32
    )


def mirror(mask, log):
    return sum(1 << (log - 1 - i) for i in range(log) if mask >> i & 1)


def call(body, outs, ins, in_specs=None, scratch=(), name=None, out_specs=None, after=None, cost=COST):
    in_specs = in_specs or [VMEM] * len(ins)
    ins = [
        pltpu.with_memory_space_constraint(a, pltpu.HBM) if spec is HBM else a
        for a, spec in zip(ins, in_specs)
    ]
    count = len(ins)
    kernel = body
    if after is not None:
        ins = ins + [after]
        in_specs = in_specs + [pl.BlockSpec(memory_space=pl.ANY)]

        def kernel(*refs):
            body(*refs[:count], *refs[count + 1 :])

    return pl.pallas_call(
        kernel,
        out_shape=[jax.ShapeDtypeStruct(s, d) for s, d in outs],
        in_specs=in_specs,
        out_specs=out_specs or [VMEM] * len(outs),
        scratch_shapes=list(scratch),
        compiler_params=pltpu.CompilerParams(vmem_limit_bytes=16 * 2**20),
        cost_estimate=cost,
        name=name,
    )(*ins)


def put_squares(out, at, squares):
    frames = squares.shape[1]
    high = squares.astype(bf16).astype(f32)
    both = jnp.concatenate([high, squares - high], axis=0).astype(bf16)
    out[at : at + SQ, :frames] = both
    if frames < out.shape[1]:
        out[at : at + SQ, frames:] = jnp.zeros((SQ, out.shape[1] - frames), bf16)


def get_squares(ref, at, frames):
    both = ref[at : at + SQ, :frames].astype(f32)
    return both[: SQ // 2] + both[SQ // 2 :]


def owner(mask):
    return lax.axis_index("mp") ^ mask


def span(start, size):
    return pl.ds(pl.multiple_of(start * size, size), size)


def cols_of(mask, side, half):
    return span(owner(mask) * 2 + side, half)


def upstream_kernel(share, masks, cot, w_depth, gain_hbm, *refs):
    *outs, up = refs[:-4]
    cot_buf, depth_buf, gain_depth, sems = refs[-4:]
    pieces = sems.shape[0] - 2
    step = depth_buf.shape[0] // pieces
    pairs = [(cot, cot_buf), (gain_hbm, gain_depth)]
    for k in range(pieces):
        rows = pl.ds(k * step, step)
        pairs.append((w_depth.at[rows, :], depth_buf.at[rows, :]))
    copies = [pltpu.make_async_copy(a, b, sems.at[i]) for i, (a, b) in enumerate(pairs)]
    for copy in copies:
        copy.start()
    copies[0].wait()
    copies[1].wait()
    for k in range(pieces):
        copies[2 + k].wait()
        cols = slice(k * step, (k + 1) * step)
        up[:, cols] = gain_depth[:, cols] * contract_last(cot_buf[...], depth_buf[cols, :])
    wide = up.shape[1] // 2
    for side, out in enumerate(outs):
        for i, mask in enumerate(masks[side]):
            out[i * share : (i + 1) * share, :] = up[
                span(owner(mask), share), side * wide : (side + 1) * wide
            ].astype(bf16)


def put_shares(share, items, up, gots, outs, first):
    wide = up.shape[1] // 2
    for side, (rows, out) in enumerate(zip(items, outs)):
        for i, (mask, places) in enumerate(rows):
            part = up[span(owner(mask), share), side * wide : (side + 1) * wide]
            for phase, at in enumerate(places):
                part = part + gots[2 * phase + side][at : at + share, :].astype(f32)
            out[first + i * share : first + (i + 1) * share, :] = part.astype(bf16)


def shares_kernel(share, items, up, *refs):
    put_shares(share, items, up, refs[:-2], refs[-2:], 0)


def join_kernel(*refs):
    for side in range(2):
        first, second, out = refs[side], refs[2 + side], refs[4 + side]
        out[: first.shape[0], :] = first[...]
        out[first.shape[0] :, :] = second[...]


def project_kernel(share, items, riders, context, w_out, *refs):
    adds, outs = refs[: -len(items)], refs[-len(items) :]
    half = outs[0].shape[1]
    frames = context.shape[0]
    at = 0
    for (mask, side, count), out in zip(items, outs):
        product = jnp.dot(
            context[...], w_out[:, cols_of(mask, side, half)], preferred_element_type=f32
        )
        for add in adds[at : at + count]:
            product = product + add[:frames, :].astype(f32)
        out[:frames, :] = product.astype(bf16)
        at += count
    if riders:
        put_shares(share, riders, adds[at], adds[at + 1 :], outs[::-1], frames)


def keep_kernel(context, w_out, residual, out):
    out[...] = residual[...].astype(f32) + jnp.dot(
        context[...],
        w_out[:, span(lax.axis_index("mp"), out.shape[1])],
        preferred_element_type=f32,
    )


def state_kernel(log, gain, w_in, kept, *refs):
    adds, (state, raw, squares, *sends) = refs[: 2 * log], refs[2 * log :]
    frames, width = state.shape
    half = width // 2
    wide = raw.shape[1] // 2
    for side in range(2):
        cols = slice(side * half, (side + 1) * half)
        total = kept[:, cols]
        for add in adds[side * log : (side + 1) * log]:
            total = total + add[:frames, :].astype(f32)
        state[:, cols] = total
    value = state[...]
    gains = gain[:, span(lax.axis_index("mp"), width)]
    raw[...] = jnp.dot((value * gains).astype(bf16), w_in[...], preferred_element_type=f32)
    column = jnp.sum(value * value, axis=1, keepdims=True)
    row = jnp.transpose(jnp.broadcast_to(column, (frames, LANES)))[: SQ // 2]
    for side, send in enumerate(sends):
        send[:frames, :] = raw[:, side * wide : (side + 1) * wide].astype(bf16)
    squares[...] = row
    put_squares(sends[0], frames, row)


def reduce_kernel(starts, held, raw, squares, *refs):
    got, own, more, (raw_out, squares_out, *sends) = refs[:2], refs[2:4], refs[4:6], refs[6:]
    frames, depth = raw.shape
    wide = depth // 2
    for side in range(2):
        cols = slice(side * wide, (side + 1) * wide)
        total = raw[:, cols] + got[side][:frames, :].astype(f32)
        raw_out[:, cols] = total
        sends[side][:frames, :] = total.astype(bf16)
        sends[side][frames : frames + held, :] = own[side][starts[0] : starts[0] + held, :]
        sends[side][frames + held : frames + 2 * held, :] = more[side][starts[1] : starts[1] + held, :]
    row = squares[...] + get_squares(got[0], got[0].shape[0] - SQ, frames)
    squares_out[...] = row
    put_squares(sends[0], frames + 2 * held, row)


def depth_rows(raw, got, rows):
    wide = raw.shape[1] // 2
    return jnp.concatenate(
        [
            raw[rows, side * wide : (side + 1) * wide] + got[side][rows, :].astype(f32)
            for side in range(2)
        ],
        axis=1,
    )


def recip_of(squares, got, frames, features):
    row = squares[...] + get_squares(got[0], got[0].shape[0] - SQ, frames)
    return jnp.transpose(
        jnp.broadcast_to(lax.rsqrt(row[:1] / features + EPS), (LANES, frames))
    )[:, :1]


def back_kernel(haves, share, features, gain, w_in, state, raw, squares, *refs):
    sent, got, (*grads, up, du) = refs[:2], refs[2:4], refs[4:]
    frames, width = state.shape
    half, wide = width // 2, raw.shape[1] // 2
    held = sent[1].shape[0] - frames
    for side in range(2):
        for i, mask in enumerate(haves[side]):
            at = i * share
            ref, at = (sent[side], at) if at < held else (got[side], at - held)
            up[span(owner(mask), share), side * wide : (side + 1) * wide] = ref[
                frames + at : frames + at + share, :
            ]
    recip = recip_of(squares, got, frames, features)
    back = []
    step = 64 if frames % 64 == 0 else frames
    for at in range(0, frames, step):
        rows = slice(at, at + step)
        depth_in = depth_rows(raw, got, rows) * recip[rows]
        upstream = up[rows, :].astype(f32)
        urecip = lax.rsqrt(jnp.mean(depth_in * depth_in, axis=1, keepdims=True) + EPS)
        inner = jnp.mean(depth_in * upstream, axis=1, keepdims=True)
        part = urecip * upstream - depth_in * (urecip * urecip * urecip * inner)
        part = part.astype(bf16)
        du[rows, :] = part
        dot_du = jnp.sum(part.astype(f32) * depth_in, axis=1, keepdims=True) / recip[rows]
        back.append(recip[rows] * recip[rows] * recip[rows] * (dot_du / features))
    back = jnp.concatenate(back, axis=0)
    gains = gain[:, span(lax.axis_index("mp"), width)]
    for side, grad in enumerate(grads):
        cols = slice(side * half, (side + 1) * half)
        dnormed = contract_last(du[...], w_in[cols, :])
        grad[...] = (recip * (gains[:, cols] * dnormed) - state[:, cols] * back).astype(bf16)


def act_kernel(features, gain_depth, w_depth, raw, squares, *refs):
    got, grads, (out, grad_out, latent) = refs[:2], refs[2:4], refs[4:]
    frames = raw.shape[0]
    half = grads[0].shape[1]
    for side in range(2):
        grad_out[:, side * half : (side + 1) * half] = grads[side][...]
    recip = recip_of(squares, got, frames, features)
    step = 64 if frames % 64 == 0 else frames
    for at in range(0, frames, step):
        rows = slice(at, at + step)
        depth_in = depth_rows(raw, got, rows) * recip[rows]
        urecip = lax.rsqrt(jnp.mean(depth_in * depth_in, axis=1, keepdims=True) + EPS)
        latent[rows, :] = (depth_in * urecip * gain_depth[...]).astype(bf16)
    out[...] = jnp.dot(latent[...], w_depth[...], preferred_element_type=f32).astype(bf16)


def context_kernel(log, items, w_out, *refs):
    blocks, rest, out = refs[: len(items)], refs[len(items) : -1], refs[-1]
    total = rest[0][...]
    for (mask, side), block in zip(items, blocks):
        part = contract_last(block[...], w_out[:, cols_of(mask, side, block.shape[1])])
        total = total + part
    out[...] = total


def own_context_kernel(log, w_out, first, second, out, *copies):
    total = None
    for side, block in enumerate((first, second)):
        half = block.shape[1]
        part = contract_last(block[...], w_out[:, cols_of(0, side, half)])
        total = part if total is None else total + part
        copies[side][...] = block[...]
    out[...] = total


def last_kernel(items, w_out, *refs):
    blocks, (total, out, buf, sems) = refs[: len(items)], refs[len(items) :]
    pieces = sems.shape[0]
    step = total.shape[1] // pieces
    copies = []
    for k in range(pieces):
        rows = slice(k * step, (k + 1) * step)
        value = total[:, rows]
        for (mask, side), block in zip(items, blocks):
            value = value + contract_last(
                block[...], w_out[rows, cols_of(mask, side, block.shape[1])]
            )
        buf[:, rows] = value.astype(bf16)
        copies.append(pltpu.make_async_copy(buf.at[:, rows], out.at[:, rows], sems.at[k]))
        copies[-1].start()
    for copy in copies:
        copy.wait()


def local(n, context, w_out, residual, gain_temporal, w_in, gain_depth, w_depth, cotangent):
    frames, width = residual.shape
    half = width // 2
    share = frames // n
    features = width * n
    heads = w_out.shape[0]
    depth, act = w_depth.shape[1:]
    wide = depth // 2
    log = n.bit_length() - 1
    bits = [1 << i for i in range(log)]
    orders = (bits, bits[::-1])
    gain = gain_temporal[None, :]

    def swap(value, bit):
        return lax.ppermute(value, "mp", [(i, i ^ bit) for i in range(n)])

    def phase_of(mask, side):
        return min(i for i, bit in enumerate(orders[side]) if mask & bit)

    masks = sorted(range(1, n), key=lambda k: (-k.bit_count(), k))
    pairs = [((k, 0), (mirror(k, log), 1)) for k in masks]

    lists = [
        [[k for k in range(1, n) if phase_of(k, side) == i] for i in range(log)]
        for side in range(2)
    ]

    def share_items(phase, gots):
        items = []
        for side, order in enumerate(orders):
            masks = lists[side][phase] if phase < log else [0]
            items.append(
                [
                    (
                        k,
                        [
                            gots[j][1] + lists[side][j].index(k ^ order[j]) * share
                            for j in range(phase)
                        ],
                    )
                    for k in masks
                ]
            )
        return items, [value for values, _ in gots for value in values]

    def shares(phase, gots, after):
        items, listed = share_items(phase, gots)
        return list(
            call(
                functools.partial(shares_kernel, share, items),
                [((share * len(items[0]), wide), bf16)] * 2,
                [up] + listed,
                name="shares",
                after=after,
                cost=FREE,
            )
        )

    def both(values, i):
        return [swap(values[side], orders[side][i]) for side in range(2)]

    *values, up = call(
        functools.partial(upstream_kernel, share, [lists[side][0] for side in range(2)]),
        [((share * n // 2, wide), bf16)] * 2 + [((frames, depth), f32)],
        [cotangent[0], w_depth[0], gain_depth],
        [HBM] * 3,
        [
            pltpu.VMEM((frames, act), bf16),
            pltpu.VMEM((depth, act), bf16),
            pltpu.VMEM((1, depth), f32),
            pltpu.SemaphoreType.DMA((3,)),
        ],
        name="upstream",
    )
    share_gots = [(both(values, 0), 0)]

    arrived = {}
    token = up
    for pair in pairs:
        items, listed, riders, extra = [], [], None, 0
        for mask, side in pair:
            phase = phase_of(mask, side)
            listed += [arrived[mask ^ bit, side] for bit in orders[side][:phase]]
            items.append((mask, side, phase))
        if log == 2 and wide == half and pair is pairs[-2]:
            riders, more = share_items(1, share_gots)
            listed += [up] + more
            extra = share * len(riders[0])
        elif log != 2 and pair is pairs[-1]:
            for i in range(1, log):
                values = shares(i, share_gots, token)
                token = values[0]
                share_gots.append((both(values, i), 0))
        values = call(
            functools.partial(project_kernel, share, items, riders),
            [((frames + extra, half), bf16)] * 2,
            [context, w_out] + listed,
            name="project",
            after=token,
        )
        token = values[0]
        for (mask, side), value in zip(pair, values):
            arrived[mask, side] = swap(value, orders[side][phase_of(mask, side)])
        if riders:
            share_gots.append(([arrived[key] for key in pair[::-1]], frames))
    kept = call(
        keep_kernel,
        [((frames, width), f32)],
        [context, w_out, residual],
        name="keep",
        after=token,
    )[0]
    own_share = shares(log, share_gots, kept)
    share_got = both(own_share, 0)

    state, raw, squares, *sends = call(
        functools.partial(state_kernel, log),
        [((frames, width), f32), ((frames, depth), f32), ((SQ // 2, frames), f32)]
        + [((frames + SQ, wide), bf16), ((frames, wide), bf16)],
        [gain, w_in, kept] + [arrived[bit, side] for side in range(2) for bit in orders[side]],
        name="state",
        after=own_share[0],
    )
    haves = [[0], [0]]
    for i in range(log):
        got = both(sends, i)
        haves = [have + [k ^ orders[s][i] for k in have] for s, have in enumerate(haves)]
        if i < log - 1:
            held = share << i
            rows = frames + 2 * held
            starts, own, more = (frames, frames), list(sends), got
            if i == 0:
                starts = (0, held)
                own = more = list(
                    call(
                        join_kernel,
                        [((2 * held, wide), bf16)] * 2,
                        own_share + share_got,
                        name="join",
                        after=squares,
                    )
                )
            raw, squares, *sends = call(
                functools.partial(reduce_kernel, starts, held),
                [(raw.shape, f32), (squares.shape, f32)]
                + [((rows + SQ, wide), bf16), ((rows, wide), bf16)],
                [raw, squares] + got + own + more,
                name="reduce",
            )
    grads = call(
        functools.partial(back_kernel, haves, share, features),
        [((frames, half), bf16)] * 2,
        [gain, w_in, state, raw, squares] + list(sends) + got,
        scratch=[pltpu.VMEM((frames, depth), bf16)] * 2,
        name="back",
    )

    total, *again = call(
        functools.partial(own_context_kernel, log),
        [((frames, heads), f32)] + [((frames, half), bf16)] * 2,
        [w_out] + list(grads),
        name="grad_context",
    )
    blocks = {(0, side): grads[side] for side in range(2)}
    for i in range(log):
        for k in range(1 << i):
            for side, order in enumerate(orders):
                mask = haves[side][k]
                value = again[side] if i and not k else blocks[mask, side]
                blocks[mask ^ order[i], side] = swap(value, order[i])

    depth_act, grad_residual = call(
        functools.partial(act_kernel, features),
        [((frames, act), bf16), ((frames, width), bf16)],
        [gain_depth, w_depth[0], raw, squares] + got + list(grads),
        scratch=[pltpu.VMEM((frames, depth), bf16)],
        name="act",
    )
    keys = [((haves[0][k], 0), (haves[1][k], 1)) for k in range(n)]
    for pair in keys[1:-1]:
        total = call(
            functools.partial(context_kernel, log, pair),
            [((frames, heads), f32)],
            [w_out] + [blocks[key] for key in pair] + [total],
            name="grad_context",
        )[0]
    grad_context = call(
        functools.partial(last_kernel, keys[-1]),
        [((frames, heads), bf16)],
        [w_out] + [blocks[key] for key in keys[-1]] + [total],
        scratch=[
            pltpu.VMEM((frames, heads), bf16),
            pltpu.SemaphoreType.DMA((min(OUT_PIECES, heads // LANES),)),
        ],
        name="grad_context",
        out_specs=[HBM],
    )[0]
    return (depth_act[None], grad_residual, grad_context)


def solution(mesh):
    in_specs = (
        P("dp", "mp"),
        P("mp", None),
        P("dp", "mp"),
        P(),
        P("mp", None),
        P("mp", None),
        P("mp", None, None),
        P("mp", "dp", None),
    )
    out_specs = (P("mp", "dp", None), P("dp", "mp"), P("dp", "mp"))
    n = mesh.shape["mp"]

    def run(*args):
        return local(n, *args)

    return jax.shard_map(run, mesh=mesh, in_specs=in_specs, out_specs=out_specs, check_vma=False)
```
